512 devices in a mesh: seq: 32 (over z, core), help: 16 (over y, x).
Axes of the slice: x: 4, y: 4, z: 16, core: 2. Of those that a mesh axis runs over, the one named last changes fastest.
Arguments:
- queries: bfloat16 [2560, 64, 640], P(('seq', 'help')), may hold values from -6 to 6
- key_rows: bfloat16 [2560, 64, 640], P(('seq', 'help')), may hold values from -6 to 6
- value_rows: bfloat16 [2560, 64, 640], P(('seq', 'help')), may hold values from -6 to 6
- grad_out: bfloat16 [2560, 64, 1280], P(('seq', 'help')), may hold values from -24 to 24
- proj_weight: bfloat16 [640, 1280], P('seq'), may hold values from -0.25 to 0.25
- proj_bias: bfloat16 [1280], P('seq'), may hold values from -3 to 3
- live_count: int32 [512], P(('seq', 'help')), may hold values from 1 to 5, as said below
Outputs:
- encoded: bfloat16 [2560, 64, 1280], P(('seq', 'help'))
- grad_queries: bfloat16 [2560, 64, 640], P(('seq', 'help'))
- grad_keys: bfloat16 [2560, 64, 640], P(('seq', 'help'))
- grad_values: bfloat16 [2560, 64, 640], P(('seq', 'help'))
- weight_grad: float32 [640, 1280], P('seq')
- bias_grad: float32 [1280], P('seq')
The draws below stay inside these ranges and needn't reach their ends.
Inputs may be any that keep to these rules, and one draw needn't show every extreme that they name: Device d's first live_count[d] slots hold image windows, its other slots are empty; some device holds 5.
All inputs are finite; a program needn't handle non-finite values.
Results may differ from the reference program's by a relative error of at most 0.04.
Values may be sent and summed in bfloat16 or wider, within the bound.
No kernel may reach another device: no remote copies, remote signals or barrier semaphores. Data moves between devices by JAX's collectives and lax.ppermute only.
A program may use at most 64 MiB of HBM per device.

```python
import jax
import jax.numpy as jnp
from jax import lax

D = 1280
H = 8
HD = 80
WIN = 64
CAP = 5
ATTN = 640
WINDOWS = 2560
N_SEQ = 32
N_HELP = 16


def draw_queries(key, part):
    key = jax.random.fold_in(key, 3)
    base = jnp.clip(jax.random.normal(key, (WINDOWS, WIN, H, HD), jnp.float32), -4.0, 4.0)
    return base.reshape(WINDOWS, WIN, H * HD).astype(jnp.bfloat16)


def draw_key_rows(key, part):
    key = jax.random.fold_in(key, 5)
    base = jnp.clip(jax.random.normal(key, (WINDOWS, WIN, H, HD), jnp.float32), -4.0, 4.0)
    return base.reshape(WINDOWS, WIN, H * HD).astype(jnp.bfloat16)


def draw_live_count(key, part):
    key = jax.random.fold_in(key, 7)
    first_key, second_key = jax.random.split(key)
    shards = N_SEQ * N_HELP
    level = jax.random.randint(first_key, (shards,), 0, 5)
    counts = jnp.where(level == 4, CAP, jnp.where(level == 3, (CAP + 1) // 2, 1)).astype(jnp.int32)
    full_at = jax.random.randint(second_key, (), 0, shards)
    return counts.at[full_at].set(CAP).astype(jnp.int32)


def with_spikes(entries, rng, source, target, blocks, factor):
    def block_of(dim):
        return (jnp.arange(entries.shape[dim]) // (entries.shape[dim] // blocks)).reshape((-1,) + (1,) * (entries.ndim - 1 - dim))

    one_side = jax.random.permutation(rng, blocks)[block_of(target)]
    second = (block_of(target) + blocks // 2) % blocks
    return jnp.where((block_of(source) == one_side) | (block_of(source) == second), factor * entries, entries)


def level_of(key, extent, cuts, low, largest):
    def one(axis_at, parts):
        steps = jax.random.uniform(jax.random.fold_in(jax.random.fold_in(key, 6), axis_at), (parts,), jnp.float32, low / len(cuts), largest / len(cuts))
        return jnp.repeat(jnp.exp(steps), extent[axis_at] // parts).reshape((-1,) + (1,) * (len(extent) - axis_at - 1))

    level = one(*cuts[0])
    for cut in cuts[1:]:
        level = level * one(*cut)
    return level


def centred(key, dims, width, limit, cuts=(), kind=jnp.bfloat16):
    level = level_of(key, dims, cuts, -0.22, 0.18) if cuts else 1.0
    array = jax.random.normal(key, dims, jnp.float32) * width * level
    return jnp.minimum(jnp.maximum(array, -limit), limit).astype(kind)


def heavy_noise(key, dims, deviation, bound, pieces, heavy, kind=jnp.bfloat16):
    values = deviation * jax.random.normal(key, dims, jnp.float32)
    if pieces:
        values = values * level_of(key, dims, pieces, -0.22, 0.18)
    return jnp.clip(with_spikes(values, jax.random.fold_in(key, 3), *heavy), -bound, bound).astype(kind)


def setup_inputs(seed: int = 0) -> dict:
    key_list = jax.random.split(jax.random.key(seed), 8)
    return {
        "queries": draw_queries(jax.random.fold_in(key_list[7], 71), 0),
        "key_rows": draw_key_rows(jax.random.fold_in(key_list[7], 71), 0),
        "value_rows": centred(key_list[2], (WINDOWS, WIN, ATTN), 1.0, 6.0, ((0, 512),)),
        "grad_out": heavy_noise(key_list[3], (WINDOWS, WIN, D), 1.0, 24.0, ((0, 512),), (0, 2, 256, 6.0)),
        "proj_weight": centred(key_list[4], (ATTN, D), ATTN ** -0.5, 0.25, ((0, 32),)),
        "proj_bias": centred(key_list[5], (D,), 0.5, 3.0, ((0, 32),)),
        "live_count": draw_live_count(jax.random.fold_in(key_list[7], 71), 0),
    }


def window_pass(query_win, key_win, value_win, grad_win, proj_weight, proj_bias):
    scale = HD ** -0.5
    query_heads = query_win.astype(jnp.float32).reshape(WIN, H, HD)
    key_heads = key_win.astype(jnp.float32).reshape(WIN, H, HD)
    value_heads = value_win.astype(jnp.float32).reshape(WIN, H, HD)
    scores = jnp.einsum('qhd,khd->hqk', query_heads, key_heads) * scale
    probs = jax.nn.softmax(scores, axis=-1)
    probs_low = probs.astype(jnp.bfloat16)
    attended = jnp.einsum('hqk,khd->qhd', probs_low.astype(jnp.float32), value_heads)
    attended = attended.reshape(WIN, H * HD).astype(jnp.bfloat16)
    encoded = (jnp.dot(attended, proj_weight, preferred_element_type=jnp.float32)
               + proj_bias.astype(jnp.float32)).astype(jnp.bfloat16)
    grad_attended = jnp.dot(grad_win, proj_weight.T, preferred_element_type=jnp.float32).astype(jnp.bfloat16)
    grad_heads = grad_attended.astype(jnp.float32).reshape(WIN, H, HD)
    attended_heads = attended.astype(jnp.float32).reshape(WIN, H, HD)
    grad_values = jnp.einsum('hqk,qhd->khd', probs_low.astype(jnp.float32), grad_heads)
    delta = jnp.einsum('qhd,qhd->hq', grad_heads, attended_heads)
    grad_probs = jnp.einsum('qhd,khd->hqk', grad_heads, value_heads)
    grad_scores = (probs * (grad_probs - delta[:, :, None])).astype(jnp.bfloat16).astype(jnp.float32)
    grad_queries = jnp.einsum('hqk,khd->qhd', grad_scores, key_heads) * scale
    grad_keys = jnp.einsum('hqk,qhd->khd', grad_scores, query_heads) * scale
    weight_term = jnp.dot(attended.T, grad_win, preferred_element_type=jnp.float32)
    bias_term = jnp.sum(grad_win.astype(jnp.float32), axis=0)
    return (encoded,
            grad_queries.reshape(WIN, H * HD).astype(jnp.bfloat16),
            grad_keys.reshape(WIN, H * HD).astype(jnp.bfloat16),
            grad_values.reshape(WIN, H * HD).astype(jnp.bfloat16),
            weight_term, bias_term)


def reference(queries, key_rows, value_rows, grad_out, proj_weight, proj_bias, live_count):
    slot_index = jnp.arange(WINDOWS, dtype=jnp.int32) % CAP
    owner_count = jnp.repeat(live_count, CAP)
    live = slot_index < owner_count

    def step(carry, inputs):
        weight_sum, bias_sum = carry
        query_win, key_win, value_win, grad_win, alive = inputs
        results = window_pass(query_win, key_win, value_win, grad_win, proj_weight, proj_bias)
        factor = jnp.where(alive, 1.0, 0.0).astype(jnp.float32)
        weight_sum = weight_sum + factor * results[4]
        bias_sum = bias_sum + factor * results[5]
        kept = tuple(jnp.where(alive, piece, jnp.zeros_like(piece)) for piece in results[:4])
        return (weight_sum, bias_sum), kept

    start = (jnp.zeros((H * HD, D), jnp.float32), jnp.zeros((D,), jnp.float32))
    (weight_grad, bias_grad), outputs = lax.scan(step, start, (queries, key_rows, value_rows, grad_out, live))
    encoded, grad_queries, grad_keys, grad_values = outputs
    return encoded, grad_queries, grad_keys, grad_values, weight_grad, bias_grad
```

```python
import jax
import jax.numpy as jnp
from jax import lax
from jax.experimental import pallas as pl
from jax.experimental.pallas import tpu as pltpu
from jax.sharding import Mesh
from jax.sharding import PartitionSpec as P

H = 8
HD = 80
WIN = 64
CAP = 5
ATTN = 640
D = 1280
Z, CORES, Y, X = 16, 2, 4, 4
SEQ = Z * CORES
HELP = Y * X
ROWS = ATTN // SEQ
BIAS = D // SEQ
BLOCKS = D // 128
PAIRS = H // 2
SPAN = 256
PART = 13
UNITS = HELP * PART
SCALE = HD**-0.5
VMEM_LIMIT = 60 * 1024 * 1024
NT = (((1,), (1,)), ((), ()))
TN = (((0,), (0,)), ((), ()))
NN = (((1,), (0,)), ((), ()))


def mm(left, right, dims):
    return lax.dot_general(left, right, dims, preferred_element_type=jnp.float32)


def head_masks(pair):
    lane = lax.broadcasted_iota(jnp.int32, (1, SPAN), 1)
    first = 32 * pair
    in_a = (lane >= first) & (lane < first + HD)
    in_b = (lane >= first + HD) & (lane < first + 2 * HD)
    return in_a.astype(jnp.float32), in_b.astype(jnp.float32)


def stacked(rows, mask_a, mask_b):
    return jnp.concatenate(
        [rows * mask_a.astype(jnp.bfloat16), rows * mask_b.astype(jnp.bfloat16)], axis=0
    )


def add_span(tiles, pair, value):
    for part in range(2):
        piece = value[:, 128 * part : 128 * (part + 1)]
        at = pair + part
        tiles[at] = piece if tiles[at] is None else tiles[at] + piece


def bias_pick():
    from_place = lax.broadcasted_iota(jnp.int32, (D, 128), 0)
    to_lane = lax.broadcasted_iota(jnp.int32, (D, 128), 1)
    return jnp.where(lax.rem(from_place, BIAS) == to_lane, 1.0, 0.0).astype(jnp.bfloat16)


def bias_owner(core):
    seq = lax.broadcasted_iota(jnp.int32, (Z, D), 0) * CORES + core
    place = lax.broadcasted_iota(jnp.int32, (Z, D), 1)
    return (place >= seq * BIAS) & (place < (seq + 1) * BIAS)


def forward_kernel(
    count_ref, core_ref, q_hbm, k_hbm, v_hbm, g_hbm, probs_hbm, att_hbm, own_hbm, other_hbm,
    q_ref, k_ref, v_ref, g_ref, probs_ref, att_ref, own_ref, other_ref, acc,
    in_sems, g_sem, out_sems, wire_sems,
):
    count, my_core = count_ref[0], core_ref[0]
    masks = [head_masks(pair) for pair in range(PAIRS)]
    moves = [
        [
            pltpu.make_async_copy(far.at[w], near.at[w], in_sems.at[which, w])
            for which, (far, near) in enumerate(((q_hbm, q_ref), (k_hbm, k_ref), (v_hbm, v_ref)))
        ]
        for w in range(CAP)
    ]
    for window_moves in moves:
        for move in window_moves:
            move.start()
    g_move = pltpu.make_async_copy(g_hbm, g_ref, g_sem)
    g_move.start()
    back = []
    for w in range(CAP):
        for move in moves[w]:
            move.wait()
        rows = slice(WIN * w, WIN * (w + 1))
        tiles = [None] * (PAIRS + 1)
        for pair in range(PAIRS):
            span = slice(128 * pair, 128 * pair + SPAN)
            mask_a, mask_b = masks[pair]
            q_both = stacked(q_ref[w, :, span], mask_a, mask_b)
            scores = mm(k_ref[w, :, span], q_both, NT) * SCALE
            raised = jnp.exp(scores - jnp.max(scores, axis=0, keepdims=True))
            probs = raised / jnp.sum(raised, axis=0, keepdims=True)
            probs_ref[w, :, 128 * pair : 128 * (pair + 1)] = probs
            both = mm(probs.astype(jnp.bfloat16), v_ref[w, :, span], TN)
            add_span(tiles, pair, both[:WIN] * mask_a + both[WIN:] * mask_b)
        keep = jnp.where(w < count, 1.0, 0.0)
        for at, tile in enumerate(tiles):
            att_ref[rows, 128 * at : 128 * (at + 1)] = (tile * keep).astype(jnp.bfloat16)
        back.append(pltpu.make_async_copy(probs_ref.at[w], probs_hbm.at[w], out_sems.at[0, w]))
        back[-1].start()
        back.append(
            pltpu.make_async_copy(
                att_ref.at[pl.ds(WIN * w, WIN)],
                att_hbm.at[pl.ds(WIN * w, WIN)],
                out_sems.at[1, w],
            )
        )
        back[-1].start()
    row_of = lax.broadcasted_iota(jnp.int32, (16, CAP * WIN), 1)
    live_rows = jnp.where(row_of < count * WIN, 1.0, 0.0).astype(jnp.bfloat16)
    left = jnp.concatenate([att_ref[...].T, live_rows], axis=0)
    g_move.wait()
    bias_parts = []
    for block in range(0, BLOCKS, 2):
        made = mm(left, g_ref[:, 128 * block : 128 * (block + 2)], NN)
        acc[block] = made[:ATTN, :128]
        acc[block + 1] = made[:ATTN, 128:]
        bias_parts.append(made[ATTN : ATTN + 1])
    bias_row = jnp.concatenate(bias_parts, axis=1)
    pick = bias_pick()
    for which, (core, wire_ref, wire_hbm) in enumerate(
        ((1 - my_core, other_ref, other_hbm), (my_core, own_ref, own_hbm))
    ):
        for row in range(ROWS):
            for block in range(BLOCKS):
                wire_ref[row * BLOCKS + block] = acc[
                    block, pl.ds(core * ROWS + row, Z, stride=CORES * ROWS), :
                ].astype(jnp.bfloat16)
        owned = jnp.where(bias_owner(core), jnp.broadcast_to(bias_row, (Z, D)), 0.0)
        wire_ref[ROWS * BLOCKS] = mm(owned.astype(jnp.bfloat16), pick, NN).astype(jnp.bfloat16)
        for unit in range(ROWS * BLOCKS + 1, UNITS):
            wire_ref[unit] = jnp.zeros((Z, 128), jnp.bfloat16)
        back.append(pltpu.make_async_copy(wire_ref, wire_hbm, wire_sems.at[which]))
        back[-1].start()
    for move in back:
        move.wait()


def backward_kernel(
    count_ref, core_ref, q_hbm, k_hbm, v_hbm, g_hbm, probs_hbm, att_hbm, near_hbm, far_hbm,
    enc_hbm, dq_hbm, dk_hbm, dv_hbm,
    q_ref, k_ref, v_ref, g_ref, probs_ref, att_ref, near_ref, far_ref,
    enc_ref, dq_ref, dk_ref, dv_ref,
    grad_att, wide, weight_ref, in_sems, out_sems, enc_sem,
):
    count, my_core = count_ref[0], core_ref[0]
    moves = [
        pltpu.make_async_copy(there, here, in_sems.at[at])
        for at, (there, here) in enumerate(
            (
                (near_hbm, near_ref), (far_hbm, far_ref), (att_hbm, att_ref), (g_hbm, g_ref),
                (v_hbm, v_ref), (probs_hbm, probs_ref), (q_hbm, q_ref), (k_hbm, k_ref),
            )
        )
    ]
    for move in moves:
        move.start()
    masks = [head_masks(pair) for pair in range(PAIRS)]
    bias_pieces = []
    for which, (held, core) in enumerate(((near_ref, my_core), (far_ref, 1 - my_core))):
        moves[which].wait()
        for unit in range(ROWS * BLOCKS + 1):
            owner, at = divmod(unit, PART)
            piece = held[owner, at]
            row, block = divmod(unit, BLOCKS)
            if row < ROWS:
                wide[block, pl.ds(core * ROWS + row, Z, stride=CORES * ROWS), :] = piece.astype(
                    jnp.float32
                )
            else:
                spread = mm(piece, bias_pick(), NT)
                bias_pieces.append(jnp.where(bias_owner(core), spread, 0.0))
    bias = jnp.sum(bias_pieces[0] + bias_pieces[1], axis=0, keepdims=True)
    for block in range(BLOCKS):
        weight_ref[:, 128 * block : 128 * (block + 1)] = wide[block].astype(jnp.bfloat16)
    moves[2].wait()
    live_rows = lax.broadcasted_iota(jnp.int32, (CAP * WIN, 1), 0) < count * WIN
    for block in range(0, BLOCKS, 2):
        cols = slice(128 * block, 128 * (block + 2))
        encoded = mm(att_ref[...], weight_ref[:, cols], NN) + bias[:, cols]
        encoded = jnp.where(live_rows, encoded, 0.0).astype(jnp.bfloat16)
        for w in range(CAP):
            enc_ref[w, :, cols] = encoded[WIN * w : WIN * (w + 1)]
    back = [pltpu.make_async_copy(enc_ref, enc_hbm, enc_sem)]
    back[0].start()
    for move in moves[3:]:
        move.wait()
    grad_att[...] = mm(g_ref[...], weight_ref[...], NT).astype(jnp.bfloat16)
    results = ((dq_ref, dq_hbm), (dk_ref, dk_hbm), (dv_ref, dv_hbm))
    for w in range(CAP):
        rows = slice(WIN * w, WIN * (w + 1))
        keep = jnp.where(w < count, 1.0, 0.0)
        dq_tiles, dk_tiles, dv_tiles = ([None] * (PAIRS + 1) for _ in range(3))
        for pair in range(PAIRS):
            span = slice(128 * pair, 128 * pair + SPAN)
            mask_a, mask_b = masks[pair]
            g_both = stacked(grad_att[rows, span], mask_a, mask_b)
            q_both = stacked(q_ref[w, :, span], mask_a, mask_b)
            grad_probs = mm(v_ref[w, :, span], g_both, NT)
            probs = probs_ref[w, :, 128 * pair : 128 * (pair + 1)]
            probs_low = probs.astype(jnp.bfloat16)
            delta = jnp.sum(probs_low.astype(jnp.float32) * grad_probs, axis=0, keepdims=True)
            grad_scores = (probs * (grad_probs - delta)).astype(jnp.bfloat16)
            add_span(dv_tiles, pair, mm(probs_low, g_both, NN))
            add_span(dk_tiles, pair, mm(grad_scores, q_both, NN))
            both = mm(grad_scores, k_ref[w, :, span], TN)
            add_span(dq_tiles, pair, both[:WIN] * mask_a + both[WIN:] * mask_b)
        for at in range(PAIRS + 1):
            cols = slice(128 * at, 128 * (at + 1))
            dq_ref[w, :, cols] = (dq_tiles[at] * (keep * SCALE)).astype(jnp.bfloat16)
            dk_ref[w, :, cols] = (dk_tiles[at] * (keep * SCALE)).astype(jnp.bfloat16)
            dv_ref[w, :, cols] = (dv_tiles[at] * keep).astype(jnp.bfloat16)
        for which, (made, out) in enumerate(results):
            move = pltpu.make_async_copy(made.at[w], out.at[w], out_sems.at[which, w])
            move.start()
            back.append(move)
    for move in back:
        move.wait()


def hbm_spec():
    return pl.BlockSpec(memory_space=pltpu.HBM)


def smem_spec():
    return pl.BlockSpec(memory_space=pltpu.SMEM)


def forward(count, core, queries, key_rows, value_rows, grads):
    return pl.pallas_call(
        forward_kernel,
        out_shape=(
            jax.ShapeDtypeStruct((CAP, WIN, H * WIN), jnp.float32),
            jax.ShapeDtypeStruct((CAP * WIN, ATTN), jnp.bfloat16),
            jax.ShapeDtypeStruct((UNITS, Z, 128), jnp.bfloat16),
            jax.ShapeDtypeStruct((UNITS, Z, 128), jnp.bfloat16),
        ),
        in_specs=[smem_spec()] * 2 + [hbm_spec()] * 4,
        out_specs=(hbm_spec(),) * 4,
        scratch_shapes=[
            pltpu.VMEM((CAP, WIN, ATTN), jnp.bfloat16),
            pltpu.VMEM((CAP, WIN, ATTN), jnp.bfloat16),
            pltpu.VMEM((CAP, WIN, ATTN), jnp.bfloat16),
            pltpu.VMEM((CAP * WIN, D), jnp.bfloat16),
            pltpu.VMEM((CAP, WIN, H * WIN), jnp.float32),
            pltpu.VMEM((CAP * WIN, ATTN), jnp.bfloat16),
            pltpu.VMEM((UNITS, Z, 128), jnp.bfloat16),
            pltpu.VMEM((UNITS, Z, 128), jnp.bfloat16),
            pltpu.VMEM((BLOCKS, ATTN, 128), jnp.float32),
            pltpu.SemaphoreType.DMA((3, CAP)),
            pltpu.SemaphoreType.DMA,
            pltpu.SemaphoreType.DMA((2, CAP)),
            pltpu.SemaphoreType.DMA((2,)),
        ],
        compiler_params=pltpu.CompilerParams(vmem_limit_bytes=VMEM_LIMIT),
        cost_estimate=pl.CostEstimate(
            flops=800_000_000, bytes_accessed=5_000_000, transcendentals=200_000
        ),
    )(count, core, queries, key_rows, value_rows, grads)


def backward(count, core, queries, key_rows, value_rows, grads, probs, attended, near, far):
    rows = jax.ShapeDtypeStruct((CAP, WIN, ATTN), jnp.bfloat16)
    return pl.pallas_call(
        backward_kernel,
        out_shape=(jax.ShapeDtypeStruct((CAP, WIN, D), jnp.bfloat16), rows, rows, rows),
        in_specs=[smem_spec()] * 2 + [hbm_spec()] * 8,
        out_specs=(hbm_spec(),) * 4,
        scratch_shapes=[
            pltpu.VMEM((CAP, WIN, ATTN), jnp.bfloat16),
            pltpu.VMEM((CAP, WIN, ATTN), jnp.bfloat16),
            pltpu.VMEM((CAP, WIN, ATTN), jnp.bfloat16),
            pltpu.VMEM((CAP * WIN, D), jnp.bfloat16),
            pltpu.VMEM((CAP, WIN, H * WIN), jnp.float32),
            pltpu.VMEM((CAP * WIN, ATTN), jnp.bfloat16),
            pltpu.VMEM((HELP, PART + 2, Z, 128), jnp.bfloat16),
            pltpu.VMEM((HELP, PART + 2, Z, 128), jnp.bfloat16),
            pltpu.VMEM((CAP, WIN, D), jnp.bfloat16),
            pltpu.VMEM((CAP, WIN, ATTN), jnp.bfloat16),
            pltpu.VMEM((CAP, WIN, ATTN), jnp.bfloat16),
            pltpu.VMEM((CAP, WIN, ATTN), jnp.bfloat16),
            pltpu.VMEM((CAP * WIN, ATTN), jnp.bfloat16),
            pltpu.VMEM((BLOCKS, ATTN, 128), jnp.float32),
            pltpu.VMEM((ATTN, D), jnp.bfloat16),
            pltpu.SemaphoreType.DMA((8,)),
            pltpu.SemaphoreType.DMA((3, CAP)),
            pltpu.SemaphoreType.DMA,
        ],
        compiler_params=pltpu.CompilerParams(vmem_limit_bytes=VMEM_LIMIT),
        cost_estimate=pl.CostEstimate(
            flops=1_500_000_000, bytes_accessed=8_000_000, transcendentals=0
        ),
    )(count, core, queries, key_rows, value_rows, grads, probs, attended, near, far)


def exchange(blocks, axis):
    return lax.all_to_all(blocks, axis, 0, 0, tiled=True)


def other_core(value):
    return lax.ppermute(value, "c", [(0, 1), (1, 0)])


def added(parts):
    return jnp.sum(parts.astype(jnp.float32), axis=0)


def own_units(proj_weight, proj_bias):
    units = jnp.concatenate(
        [
            proj_weight.reshape(ROWS * BLOCKS, 128),
            jnp.pad(proj_bias, (0, 128 - BIAS))[None],
            jnp.zeros((UNITS - ROWS * BLOCKS - 1, 128), jnp.bfloat16),
        ],
        axis=0,
    )
    mine = lax.axis_index("y") * X + lax.axis_index("x")
    return lax.dynamic_index_in_dim(units.reshape(HELP, PART, 128), mine, 0, keepdims=False)


def on_device(queries, key_rows, value_rows, grad_out, proj_weight, proj_bias, live_count):
    core = lax.axis_index("c").reshape(1)
    grads = grad_out.reshape(CAP * WIN, D)
    share = own_units(proj_weight, proj_bias)
    probs, attended, own, other = forward(live_count, core, queries, key_rows, value_rows, grads)
    both = added(jnp.stack([own, other_core(other)])).astype(jnp.bfloat16)
    over_help = exchange(both.reshape(HELP, PART, Z, 128), ("y", "x"))
    part = added(over_help).astype(jnp.bfloat16).transpose(1, 0, 2)
    shares = jnp.broadcast_to(share[None], (Z, PART, 128))
    over_z = exchange(jnp.concatenate([part, shares], axis=1), "z")
    whole = added(over_z[:, :PART])
    high = whole.astype(jnp.bfloat16)
    low = (whole - high.astype(jnp.float32)).astype(jnp.bfloat16)
    ends = jnp.pad(jnp.stack([high, low]), ((0, 0), (0, Z - PART), (0, 0)))
    sent = jnp.concatenate([over_z[:, PART:].transpose(1, 0, 2), ends], axis=0)
    near = exchange(jnp.broadcast_to(sent[None], (HELP, PART + 2, Z, 128)), ("y", "x"))
    encoded, grad_queries, grad_keys, grad_values = backward(
        live_count, core, queries, key_rows, value_rows, grads, probs, attended, near,
        other_core(near),
    )
    units = near[:, PART, :PART].astype(jnp.float32) + near[:, PART + 1, :PART].astype(jnp.float32)
    units = units.reshape(UNITS, 128)
    weight_grad = units[: ROWS * BLOCKS].reshape(ROWS, D)
    bias_grad = units[ROWS * BLOCKS, :BIAS]
    return (encoded, grad_queries, grad_keys, grad_values, weight_grad, bias_grad)


def solution(mesh):
    torus = Mesh(mesh.devices.reshape(Z, CORES, Y, X), ("z", "c", "y", "x"))
    windows = P(("z", "c", "y", "x"), None, None)
    lines, line = P(("z", "c"), None), P(("z", "c"))
    return jax.shard_map(
        on_device,
        mesh=torus,
        in_specs=(windows, windows, windows, windows, lines, line, P(("z", "c", "y", "x"))),
        out_specs=(windows, windows, windows, windows, lines, line),
        check_vma=False,
    )
```

```python
import jax
import jax.numpy as jnp
from jax import lax
from jax.experimental import pallas as pl
from jax.experimental.pallas import tpu as pltpu
from jax.sharding import Mesh
from jax.sharding import PartitionSpec as P

H = 8
HD = 80
WIN = 64
CAP = 5
ATTN = 640
D = 1280
Z, CORES, Y, X = 16, 2, 4, 4
SEQ = Z * CORES
HELP = Y * X
ROWS = ATTN // SEQ
BIAS = D // SEQ
BLOCKS = D // 128
PAIRS = H // 2
SPAN = 256
PART = 13
UNITS = HELP * PART
SCALE = HD**-0.5
VMEM_LIMIT = 24 * 1024 * 1024
NT = (((1,), (1,)), ((), ()))
TN = (((0,), (0,)), ((), ()))
NN = (((1,), (0,)), ((), ()))


def mm(left, right, dims):
    return lax.dot_general(left, right, dims, preferred_element_type=jnp.float32)


def head_masks(pair):
    lane = lax.broadcasted_iota(jnp.int32, (1, SPAN), 1)
    first = 32 * pair
    in_a = (lane >= first) & (lane < first + HD)
    in_b = (lane >= first + HD) & (lane < first + 2 * HD)
    return in_a.astype(jnp.float32), in_b.astype(jnp.float32)


def stacked(rows, mask_a, mask_b):
    return jnp.concatenate(
        [rows * mask_a.astype(jnp.bfloat16), rows * mask_b.astype(jnp.bfloat16)], axis=0
    )


def add_span(tiles, pair, value):
    for part in range(2):
        piece = value[:, 128 * part : 128 * (part + 1)]
        at = pair + part
        tiles[at] = piece if tiles[at] is None else tiles[at] + piece


def bias_pick():
    from_place = lax.broadcasted_iota(jnp.int32, (D, 128), 0)
    to_lane = lax.broadcasted_iota(jnp.int32, (D, 128), 1)
    return jnp.where(lax.rem(from_place, BIAS) == to_lane, 1.0, 0.0).astype(jnp.bfloat16)


def bias_owner(core):
    seq = lax.broadcasted_iota(jnp.int32, (Z, D), 0) * CORES + core
    place = lax.broadcasted_iota(jnp.int32, (Z, D), 1)
    return (place >= seq * BIAS) & (place < (seq + 1) * BIAS)


def forward_kernel(
    count_ref, core_ref, q_hbm, k_hbm, v_hbm, g_hbm, probs_ref, att_ref, own_ref, other_ref,
    q_ref, k_ref, v_ref, g_ref, acc, in_sems, g_sem,
):
    count, my_core = count_ref[0], core_ref[0]
    masks = [head_masks(pair) for pair in range(PAIRS)]
    moves = [
        [
            pltpu.make_async_copy(far.at[w], near.at[w], in_sems.at[which, w])
            for which, (far, near) in enumerate(((q_hbm, q_ref), (k_hbm, k_ref), (v_hbm, v_ref)))
        ]
        for w in range(CAP)
    ]
    for window_moves in moves:
        for move in window_moves:
            move.start()
    g_move = pltpu.make_async_copy(g_hbm, g_ref, g_sem)
    g_move.start()
    for w in range(CAP):
        for move in moves[w]:
            move.wait()
        rows = slice(WIN * w, WIN * (w + 1))
        tiles = [None] * (PAIRS + 1)
        for pair in range(PAIRS):
            span = slice(128 * pair, 128 * pair + SPAN)
            mask_a, mask_b = masks[pair]
            q_both = stacked(q_ref[w, :, span], mask_a, mask_b)
            scores = mm(k_ref[w, :, span], q_both, NT) * SCALE
            raised = jnp.exp(scores - jnp.max(scores, axis=0, keepdims=True))
            probs = raised / jnp.sum(raised, axis=0, keepdims=True)
            probs_ref[w, :, 128 * pair : 128 * (pair + 1)] = probs
            both = mm(probs.astype(jnp.bfloat16), v_ref[w, :, span], TN)
            add_span(tiles, pair, both[:WIN] * mask_a + both[WIN:] * mask_b)
        keep = jnp.where(w < count, 1.0, 0.0)
        for at, tile in enumerate(tiles):
            att_ref[rows, 128 * at : 128 * (at + 1)] = (tile * keep).astype(jnp.bfloat16)
    row_of = lax.broadcasted_iota(jnp.int32, (16, CAP * WIN), 1)
    live_rows = jnp.where(row_of < count * WIN, 1.0, 0.0).astype(jnp.bfloat16)
    left = jnp.concatenate([att_ref[...].T, live_rows], axis=0)
    g_move.wait()
    bias_parts = []
    for block in range(0, BLOCKS, 2):
        made = mm(left, g_ref[:, 128 * block : 128 * (block + 2)], NN)
        acc[block] = made[:ATTN, :128]
        acc[block + 1] = made[:ATTN, 128:]
        bias_parts.append(made[ATTN : ATTN + 1])
    bias_row = jnp.concatenate(bias_parts, axis=1)
    pick = bias_pick()
    for core, wire_ref in ((my_core, own_ref), (1 - my_core, other_ref)):
        for row in range(ROWS):
            for block in range(BLOCKS):
                wire_ref[row * BLOCKS + block] = acc[
                    block, pl.ds(core * ROWS + row, Z, stride=CORES * ROWS), :
                ].astype(jnp.bfloat16)
        owned = jnp.where(bias_owner(core), jnp.broadcast_to(bias_row, (Z, D)), 0.0)
        wire_ref[ROWS * BLOCKS] = mm(owned.astype(jnp.bfloat16), pick, NN).astype(jnp.bfloat16)
        for unit in range(ROWS * BLOCKS + 1, UNITS):
            wire_ref[unit] = jnp.zeros((Z, 128), jnp.bfloat16)


def backward_kernel(
    count_ref, core_ref, q_hbm, k_hbm, v_hbm, g_hbm, probs_ref, att_ref, near_ref, far_ref,
    enc_hbm, dq_hbm, dk_hbm, dv_hbm,
    q_ref, k_ref, v_ref, g_ref, enc_ref, dq_ref, dk_ref, dv_ref,
    grad_att, wide, weight_ref, in_sems, out_sems, enc_sem,
):
    count, my_core = count_ref[0], core_ref[0]
    moves = [
        pltpu.make_async_copy(there, here, in_sems.at[at])
        for at, (there, here) in enumerate(
            ((g_hbm, g_ref), (v_hbm, v_ref), (q_hbm, q_ref), (k_hbm, k_ref))
        )
    ]
    for move in moves:
        move.start()
    masks = [head_masks(pair) for pair in range(PAIRS)]
    bias_pieces = []
    for held, core in ((near_ref, my_core), (far_ref, 1 - my_core)):
        for unit in range(ROWS * BLOCKS + 1):
            owner, at = divmod(unit, PART)
            piece = held[owner, at]
            row, block = divmod(unit, BLOCKS)
            if row < ROWS:
                wide[block, pl.ds(core * ROWS + row, Z, stride=CORES * ROWS), :] = piece.astype(
                    jnp.float32
                )
            else:
                spread = mm(piece, bias_pick(), NT)
                bias_pieces.append(jnp.where(bias_owner(core), spread, 0.0))
    bias = jnp.sum(bias_pieces[0] + bias_pieces[1], axis=0, keepdims=True)
    for block in range(BLOCKS):
        weight_ref[:, 128 * block : 128 * (block + 1)] = wide[block].astype(jnp.bfloat16)
    live_rows = lax.broadcasted_iota(jnp.int32, (CAP * WIN, 1), 0) < count * WIN
    for block in range(0, BLOCKS, 2):
        cols = slice(128 * block, 128 * (block + 2))
        encoded = mm(att_ref[...], weight_ref[:, cols], NN) + bias[:, cols]
        encoded = jnp.where(live_rows, encoded, 0.0).astype(jnp.bfloat16)
        for w in range(CAP):
            enc_ref[w, :, cols] = encoded[WIN * w : WIN * (w + 1)]
    back = [pltpu.make_async_copy(enc_ref, enc_hbm, enc_sem)]
    back[0].start()
    for move in moves:
        move.wait()
    grad_att[...] = mm(g_ref[...], weight_ref[...], NT).astype(jnp.bfloat16)
    results = ((dq_ref, dq_hbm), (dk_ref, dk_hbm), (dv_ref, dv_hbm))
    for w in range(CAP):
        rows = slice(WIN * w, WIN * (w + 1))
        keep = jnp.where(w < count, 1.0, 0.0)
        dq_tiles, dk_tiles, dv_tiles = ([None] * (PAIRS + 1) for _ in range(3))
        for pair in range(PAIRS):
            span = slice(128 * pair, 128 * pair + SPAN)
            mask_a, mask_b = masks[pair]
            g_both = stacked(grad_att[rows, span], mask_a, mask_b)
            q_both = stacked(q_ref[w, :, span], mask_a, mask_b)
            grad_probs = mm(v_ref[w, :, span], g_both, NT)
            probs = probs_ref[w, :, 128 * pair : 128 * (pair + 1)]
            probs_low = probs.astype(jnp.bfloat16)
            delta = jnp.sum(probs_low.astype(jnp.float32) * grad_probs, axis=0, keepdims=True)
            grad_scores = (probs * (grad_probs - delta)).astype(jnp.bfloat16)
            add_span(dv_tiles, pair, mm(probs_low, g_both, NN))
            add_span(dk_tiles, pair, mm(grad_scores, q_both, NN))
            both = mm(grad_scores, k_ref[w, :, span], TN)
            add_span(dq_tiles, pair, both[:WIN] * mask_a + both[WIN:] * mask_b)
        for at in range(PAIRS + 1):
            cols = slice(128 * at, 128 * (at + 1))
            dq_ref[w, :, cols] = (dq_tiles[at] * (keep * SCALE)).astype(jnp.bfloat16)
            dk_ref[w, :, cols] = (dk_tiles[at] * (keep * SCALE)).astype(jnp.bfloat16)
            dv_ref[w, :, cols] = (dv_tiles[at] * keep).astype(jnp.bfloat16)
        for which, (made, out) in enumerate(results):
            move = pltpu.make_async_copy(made.at[w], out.at[w], out_sems.at[which, w])
            move.start()
            back.append(move)
    for move in back:
        move.wait()


def in_hbm(value):
    return pltpu.with_memory_space_constraint(value, pltpu.HBM)


def in_vmem(value):
    return pltpu.with_memory_space_constraint(value, pltpu.VMEM)


def vmem_spec():
    return pl.BlockSpec(memory_space=pltpu.VMEM)


def hbm_spec():
    return pl.BlockSpec(memory_space=pltpu.HBM)


def smem_spec():
    return pl.BlockSpec(memory_space=pltpu.SMEM)


def forward(count, core, queries, key_rows, value_rows, grads):
    return pl.pallas_call(
        forward_kernel,
        out_shape=(
            pltpu.VMEM((CAP, WIN, H * WIN), jnp.float32),
            pltpu.VMEM((CAP * WIN, ATTN), jnp.bfloat16),
            pltpu.VMEM((UNITS, Z, 128), jnp.bfloat16),
            pltpu.VMEM((UNITS, Z, 128), jnp.bfloat16),
        ),
        in_specs=[smem_spec()] * 2 + [hbm_spec()] * 4,
        out_specs=(vmem_spec(),) * 4,
        scratch_shapes=[
            pltpu.VMEM((CAP, WIN, ATTN), jnp.bfloat16),
            pltpu.VMEM((CAP, WIN, ATTN), jnp.bfloat16),
            pltpu.VMEM((CAP, WIN, ATTN), jnp.bfloat16),
            pltpu.VMEM((CAP * WIN, D), jnp.bfloat16),
            pltpu.VMEM((BLOCKS, ATTN, 128), jnp.float32),
            pltpu.SemaphoreType.DMA((3, CAP)),
            pltpu.SemaphoreType.DMA,
        ],
        compiler_params=pltpu.CompilerParams(vmem_limit_bytes=VMEM_LIMIT),
        cost_estimate=pl.CostEstimate(
            flops=800_000_000, bytes_accessed=5_000_000, transcendentals=200_000
        ),
    )(count, core, *(in_hbm(array) for array in (queries, key_rows, value_rows, grads)))


def backward(count, core, queries, key_rows, value_rows, grads, probs, attended, near, far):
    rows = jax.ShapeDtypeStruct((CAP, WIN, ATTN), jnp.bfloat16)
    return pl.pallas_call(
        backward_kernel,
        out_shape=(jax.ShapeDtypeStruct((CAP, WIN, D), jnp.bfloat16), rows, rows, rows),
        in_specs=[smem_spec()] * 2 + [hbm_spec()] * 4 + [vmem_spec()] * 4,
        out_specs=(hbm_spec(),) * 4,
        scratch_shapes=[
            pltpu.VMEM((CAP, WIN, ATTN), jnp.bfloat16),
            pltpu.VMEM((CAP, WIN, ATTN), jnp.bfloat16),
            pltpu.VMEM((CAP, WIN, ATTN), jnp.bfloat16),
            pltpu.VMEM((CAP * WIN, D), jnp.bfloat16),
            pltpu.VMEM((CAP, WIN, D), jnp.bfloat16),
            pltpu.VMEM((CAP, WIN, ATTN), jnp.bfloat16),
            pltpu.VMEM((CAP, WIN, ATTN), jnp.bfloat16),
            pltpu.VMEM((CAP, WIN, ATTN), jnp.bfloat16),
            pltpu.VMEM((CAP * WIN, ATTN), jnp.bfloat16),
            pltpu.VMEM((BLOCKS, ATTN, 128), jnp.float32),
            pltpu.VMEM((ATTN, D), jnp.bfloat16),
            pltpu.SemaphoreType.DMA((4,)),
            pltpu.SemaphoreType.DMA((3, CAP)),
            pltpu.SemaphoreType.DMA,
        ],
        compiler_params=pltpu.CompilerParams(vmem_limit_bytes=VMEM_LIMIT),
        cost_estimate=pl.CostEstimate(
            flops=1_500_000_000, bytes_accessed=8_000_000, transcendentals=0
        ),
    )(
        count, core, *(in_hbm(array) for array in (queries, key_rows, value_rows, grads)),
        *(in_vmem(array) for array in (probs, attended, near, far)),
    )


def exchange(blocks, axis):
    return lax.all_to_all(blocks, axis, 0, 0, tiled=True)


def other_core(value):
    return lax.ppermute(value, "c", [(0, 1), (1, 0)])


def added(parts):
    return jnp.sum(parts.astype(jnp.float32), axis=0)


def own_units(proj_weight, proj_bias):
    units = jnp.concatenate(
        [
            proj_weight.reshape(ROWS * BLOCKS, 128),
            jnp.pad(proj_bias, (0, 128 - BIAS))[None],
            jnp.zeros((UNITS - ROWS * BLOCKS - 1, 128), jnp.bfloat16),
        ],
        axis=0,
    )
    mine = lax.axis_index("y") * X + lax.axis_index("x")
    return lax.dynamic_index_in_dim(units.reshape(HELP, PART, 128), mine, 0, keepdims=False)


def on_device(queries, key_rows, value_rows, grad_out, proj_weight, proj_bias, live_count):
    core = lax.axis_index("c").reshape(1)
    grads = grad_out.reshape(CAP * WIN, D)
    share = own_units(proj_weight, proj_bias)
    probs, attended, own, other = forward(live_count, core, queries, key_rows, value_rows, grads)
    both = added(jnp.stack([own, other_core(other)])).astype(jnp.bfloat16)
    over_help = exchange(both.reshape(HELP, PART, Z, 128), ("y", "x"))
    part = added(over_help).astype(jnp.bfloat16).transpose(1, 0, 2)
    shares = jnp.broadcast_to(share[None], (Z, PART, 128))
    over_z = exchange(jnp.concatenate([part, shares], axis=1), "z")
    whole = added(over_z[:, :PART])
    high = whole.astype(jnp.bfloat16)
    low = (whole - high.astype(jnp.float32)).astype(jnp.bfloat16)
    ends = jnp.pad(jnp.stack([high, low]), ((0, 0), (0, Z - PART), (0, 0)))
    sent = jnp.concatenate([over_z[:, PART:].transpose(1, 0, 2), ends], axis=0)
    near = exchange(jnp.broadcast_to(sent[None], (HELP, PART + 2, Z, 128)), ("y", "x"))
    encoded, grad_queries, grad_keys, grad_values = backward(
        live_count, core, queries, key_rows, value_rows, grads, probs, attended, near,
        other_core(near),
    )
    units = near[:, PART, :PART].astype(jnp.float32) + near[:, PART + 1, :PART].astype(jnp.float32)
    units = units.reshape(UNITS, 128)
    weight_grad = units[: ROWS * BLOCKS].reshape(ROWS, D)
    bias_grad = units[ROWS * BLOCKS, :BIAS]
    return (encoded, grad_queries, grad_keys, grad_values, weight_grad, bias_grad)


def solution(mesh):
    torus = Mesh(mesh.devices.reshape(Z, CORES, Y, X), ("z", "c", "y", "x"))
    windows = P(("z", "c", "y", "x"), None, None)
    lines, line = P(("z", "c"), None), P(("z", "c"))
    return jax.shard_map(
        on_device,
        mesh=torus,
        in_specs=(windows, windows, windows, windows, lines, line, P(("z", "c", "y", "x"))),
        out_specs=(windows, windows, windows, windows, lines, line),
        check_vma=False,
    )
```

```python
import jax
import jax.numpy as jnp
from jax import lax
from jax.experimental import pallas as pl
from jax.experimental.pallas import tpu as pltpu
from jax.sharding import Mesh
from jax.sharding import PartitionSpec as P

H = 8
HD = 80
WIN = 64
CAP = 5
ATTN = 640
D = 1280
Z, CORES, Y, X = 16, 2, 4, 4
SEQ = Z * CORES
HELP = Y * X
ROWS = ATTN // SEQ
BIAS = D // SEQ
BLOCKS = D // 128
PAIRS = H // 2
SPAN = 256
PART = 13
UNITS = HELP * PART
SCALE = HD**-0.5
VMEM_LIMIT = 24 * 1024 * 1024
NT = (((1,), (1,)), ((), ()))
TN = (((0,), (0,)), ((), ()))
NN = (((1,), (0,)), ((), ()))


def mm(left, right, dims):
    return lax.dot_general(left, right, dims, preferred_element_type=jnp.float32)


def head_masks(pair):
    lane = lax.broadcasted_iota(jnp.int32, (1, SPAN), 1)
    first = 32 * pair
    in_a = (lane >= first) & (lane < first + HD)
    in_b = (lane >= first + HD) & (lane < first + 2 * HD)
    return in_a.astype(jnp.float32), in_b.astype(jnp.float32)


def stacked(rows, mask_a, mask_b):
    return jnp.concatenate(
        [rows * mask_a.astype(jnp.bfloat16), rows * mask_b.astype(jnp.bfloat16)], axis=0
    )


def add_span(tiles, pair, value):
    for part in range(2):
        piece = value[:, 128 * part : 128 * (part + 1)]
        at = pair + part
        tiles[at] = piece if tiles[at] is None else tiles[at] + piece


def bias_pick():
    from_place = lax.broadcasted_iota(jnp.int32, (D, 128), 0)
    to_lane = lax.broadcasted_iota(jnp.int32, (D, 128), 1)
    owner = (from_place * 1639) >> 16
    return jnp.where(from_place - owner * BIAS == to_lane, 1.0, 0.0).astype(jnp.bfloat16)


def bias_owner(core):
    seq = lax.broadcasted_iota(jnp.int32, (Z, D), 0) * CORES + core
    place = lax.broadcasted_iota(jnp.int32, (Z, D), 1)
    return (place >= seq * BIAS) & (place < (seq + 1) * BIAS)


def forward_kernel(
    count_ref, core_ref, q_hbm, k_hbm, v_hbm, g_hbm, probs_ref, att_ref, own_ref, other_ref,
    q_ref, k_ref, v_ref, g_ref, acc, in_sems,
):
    count, my_core = count_ref[0], core_ref[0]
    masks = [head_masks(pair) for pair in range(PAIRS)]
    moves = [
        pltpu.make_async_copy(there, here, in_sems.at[at])
        for at, (there, here) in enumerate(
            ((q_hbm, q_ref), (k_hbm, k_ref), (v_hbm, v_ref), (g_hbm, g_ref))
        )
    ]
    for move in moves:
        move.start()
    for move in moves[:3]:
        move.wait()
    for w in range(CAP):
        rows = slice(WIN * w, WIN * (w + 1))
        tiles = [None] * (PAIRS + 1)
        for pair in range(PAIRS):
            span = slice(128 * pair, 128 * pair + SPAN)
            mask_a, mask_b = masks[pair]
            q_both = stacked(q_ref[w, :, span], mask_a, mask_b)
            scores = mm(k_ref[w, :, span], q_both, NT) * SCALE
            raised = jnp.exp(scores - jnp.max(scores, axis=0, keepdims=True))
            probs = raised * (1.0 / jnp.sum(raised, axis=0, keepdims=True))
            probs_ref[w, :, 128 * pair : 128 * (pair + 1)] = probs
            both = mm(probs.astype(jnp.bfloat16), v_ref[w, :, span], TN)
            add_span(tiles, pair, both[:WIN] * mask_a + both[WIN:] * mask_b)
        keep = jnp.where(w < count, 1.0, 0.0)
        for at, tile in enumerate(tiles):
            att_ref[rows, 128 * at : 128 * (at + 1)] = (tile * keep).astype(jnp.bfloat16)
    row_of = lax.broadcasted_iota(jnp.int32, (16, CAP * WIN), 1)
    live_rows = jnp.where(row_of < count * WIN, 1.0, 0.0).astype(jnp.bfloat16)
    left = jnp.concatenate([att_ref[...].T, live_rows], axis=0)
    moves[3].wait()
    bias_parts = []
    for block in range(0, BLOCKS, 2):
        made = mm(left, g_ref[:, 128 * block : 128 * (block + 2)], NN)
        acc[block] = made[:ATTN, :128]
        acc[block + 1] = made[:ATTN, 128:]
        bias_parts.append(made[ATTN : ATTN + 1])
    bias_row = jnp.concatenate(bias_parts, axis=1)
    pick = bias_pick()
    for core, wire_ref in ((my_core, own_ref), (1 - my_core, other_ref)):
        for row in range(ROWS):
            for block in range(BLOCKS):
                wire_ref[row * BLOCKS + block] = acc[
                    block, pl.ds(core * ROWS + row, Z, stride=CORES * ROWS), :
                ].astype(jnp.bfloat16)
        owned = jnp.where(bias_owner(core), jnp.broadcast_to(bias_row, (Z, D)), 0.0)
        wire_ref[ROWS * BLOCKS] = mm(owned.astype(jnp.bfloat16), pick, NN).astype(jnp.bfloat16)
        for unit in range(ROWS * BLOCKS + 1, UNITS):
            wire_ref[unit] = jnp.zeros((Z, 128), jnp.bfloat16)


def backward_kernel(
    count_ref, core_ref, q_hbm, k_hbm, v_hbm, g_hbm, probs_ref, att_ref, near_ref, far_ref,
    enc_hbm, dq_hbm, dk_hbm, dv_hbm,
    q_ref, k_ref, v_ref, g_ref, enc_ref, dq_ref, dk_ref, dv_ref,
    grad_att, wide, weight_ref, in_sems, out_sems, enc_sem,
):
    count, my_core = count_ref[0], core_ref[0]
    moves = [
        pltpu.make_async_copy(there, here, in_sems.at[at])
        for at, (there, here) in enumerate(
            ((g_hbm, g_ref), (v_hbm, v_ref), (q_hbm, q_ref), (k_hbm, k_ref))
        )
    ]
    for move in moves:
        move.start()
    masks = [head_masks(pair) for pair in range(PAIRS)]
    bias_pieces = []
    for held, core in ((near_ref, my_core), (far_ref, 1 - my_core)):
        for unit in range(ROWS * BLOCKS + 1):
            owner, at = divmod(unit, PART)
            piece = held[owner, at]
            row, block = divmod(unit, BLOCKS)
            if row < ROWS:
                wide[block, pl.ds(core * ROWS + row, Z, stride=CORES * ROWS), :] = piece.astype(
                    jnp.float32
                )
            else:
                spread = mm(piece, bias_pick(), NT)
                bias_pieces.append(jnp.where(bias_owner(core), spread, 0.0))
    bias = jnp.sum(bias_pieces[0] + bias_pieces[1], axis=0, keepdims=True)
    for block in range(BLOCKS):
        weight_ref[:, 128 * block : 128 * (block + 1)] = wide[block].astype(jnp.bfloat16)
    live_rows = lax.broadcasted_iota(jnp.int32, (CAP * WIN, 1), 0) < count * WIN
    for block in range(0, BLOCKS, 2):
        cols = slice(128 * block, 128 * (block + 2))
        encoded = mm(att_ref[...], weight_ref[:, cols], NN) + bias[:, cols]
        encoded = jnp.where(live_rows, encoded, 0.0).astype(jnp.bfloat16)
        for w in range(CAP):
            enc_ref[w, :, cols] = encoded[WIN * w : WIN * (w + 1)]
    back = [pltpu.make_async_copy(enc_ref, enc_hbm, enc_sem)]
    back[0].start()
    for move in moves:
        move.wait()
    grad_att[...] = mm(g_ref[...], weight_ref[...], NT).astype(jnp.bfloat16)
    for w in range(CAP):
        rows = slice(WIN * w, WIN * (w + 1))
        keep = jnp.where(w < count, 1.0, 0.0)
        dq_tiles, dk_tiles, dv_tiles = ([None] * (PAIRS + 1) for _ in range(3))
        for pair in range(PAIRS):
            span = slice(128 * pair, 128 * pair + SPAN)
            mask_a, mask_b = masks[pair]
            g_both = stacked(grad_att[rows, span], mask_a, mask_b)
            q_both = stacked(q_ref[w, :, span], mask_a, mask_b)
            grad_probs = mm(v_ref[w, :, span], g_both, NT)
            probs = probs_ref[w, :, 128 * pair : 128 * (pair + 1)]
            probs_low = probs.astype(jnp.bfloat16)
            delta = jnp.sum(probs_low.astype(jnp.float32) * grad_probs, axis=0, keepdims=True)
            grad_scores = (probs * (grad_probs - delta)).astype(jnp.bfloat16)
            add_span(dv_tiles, pair, mm(probs_low, g_both, NN))
            add_span(dk_tiles, pair, mm(grad_scores, q_both, NN))
            both = mm(grad_scores, k_ref[w, :, span], TN)
            add_span(dq_tiles, pair, both[:WIN] * mask_a + both[WIN:] * mask_b)
        for at in range(PAIRS + 1):
            cols = slice(128 * at, 128 * (at + 1))
            dq_ref[w, :, cols] = (dq_tiles[at] * (keep * SCALE)).astype(jnp.bfloat16)
            dk_ref[w, :, cols] = (dk_tiles[at] * (keep * SCALE)).astype(jnp.bfloat16)
            dv_ref[w, :, cols] = (dv_tiles[at] * keep).astype(jnp.bfloat16)
    results = ((dq_ref, dq_hbm), (dk_ref, dk_hbm), (dv_ref, dv_hbm))
    for which, (made, out) in enumerate(results):
        back.append(pltpu.make_async_copy(made, out, out_sems.at[which]))
        back[-1].start()
    for move in back:
        move.wait()


def in_hbm(value):
    return pltpu.with_memory_space_constraint(value, pltpu.HBM)


def in_vmem(value):
    return pltpu.with_memory_space_constraint(value, pltpu.VMEM)


def vmem_spec():
    return pl.BlockSpec(memory_space=pltpu.VMEM)


def hbm_spec():
    return pl.BlockSpec(memory_space=pltpu.HBM)


def smem_spec():
    return pl.BlockSpec(memory_space=pltpu.SMEM)


def forward(count, core, queries, key_rows, value_rows, grads):
    return pl.pallas_call(
        forward_kernel,
        out_shape=(
            pltpu.VMEM((CAP, WIN, H * WIN), jnp.float32),
            pltpu.VMEM((CAP * WIN, ATTN), jnp.bfloat16),
            pltpu.VMEM((UNITS, Z, 128), jnp.bfloat16),
            pltpu.VMEM((UNITS, Z, 128), jnp.bfloat16),
        ),
        in_specs=[smem_spec()] * 2 + [hbm_spec()] * 4,
        out_specs=(vmem_spec(),) * 4,
        scratch_shapes=[
            pltpu.VMEM((CAP, WIN, ATTN), jnp.bfloat16),
            pltpu.VMEM((CAP, WIN, ATTN), jnp.bfloat16),
            pltpu.VMEM((CAP, WIN, ATTN), jnp.bfloat16),
            pltpu.VMEM((CAP * WIN, D), jnp.bfloat16),
            pltpu.VMEM((BLOCKS, ATTN, 128), jnp.float32),
            pltpu.SemaphoreType.DMA((4,)),
        ],
        compiler_params=pltpu.CompilerParams(vmem_limit_bytes=VMEM_LIMIT),
        cost_estimate=pl.CostEstimate(
            flops=800_000_000, bytes_accessed=5_000_000, transcendentals=200_000
        ),
    )(count, core, *(in_hbm(array) for array in (queries, key_rows, value_rows, grads)))


def backward(count, core, queries, key_rows, value_rows, grads, probs, attended, near, far):
    rows = jax.ShapeDtypeStruct((CAP, WIN, ATTN), jnp.bfloat16)
    return pl.pallas_call(
        backward_kernel,
        out_shape=(jax.ShapeDtypeStruct((CAP, WIN, D), jnp.bfloat16), rows, rows, rows),
        in_specs=[smem_spec()] * 2 + [hbm_spec()] * 4 + [vmem_spec()] * 4,
        out_specs=(hbm_spec(),) * 4,
        scratch_shapes=[
            pltpu.VMEM((CAP, WIN, ATTN), jnp.bfloat16),
            pltpu.VMEM((CAP, WIN, ATTN), jnp.bfloat16),
            pltpu.VMEM((CAP, WIN, ATTN), jnp.bfloat16),
            pltpu.VMEM((CAP * WIN, D), jnp.bfloat16),
            pltpu.VMEM((CAP, WIN, D), jnp.bfloat16),
            pltpu.VMEM((CAP, WIN, ATTN), jnp.bfloat16),
            pltpu.VMEM((CAP, WIN, ATTN), jnp.bfloat16),
            pltpu.VMEM((CAP, WIN, ATTN), jnp.bfloat16),
            pltpu.VMEM((CAP * WIN, ATTN), jnp.bfloat16),
            pltpu.VMEM((BLOCKS, ATTN, 128), jnp.float32),
            pltpu.VMEM((ATTN, D), jnp.bfloat16),
            pltpu.SemaphoreType.DMA((4,)),
            pltpu.SemaphoreType.DMA((3,)),
            pltpu.SemaphoreType.DMA,
        ],
        compiler_params=pltpu.CompilerParams(vmem_limit_bytes=VMEM_LIMIT),
        cost_estimate=pl.CostEstimate(
            flops=1_500_000_000, bytes_accessed=8_000_000, transcendentals=0
        ),
    )(
        count, core, *(in_hbm(array) for array in (queries, key_rows, value_rows, grads)),
        *(in_vmem(array) for array in (probs, attended, near, far)),
    )


def exchange(blocks, axis):
    return lax.all_to_all(blocks, axis, 0, 0, tiled=True)


def other_core(value):
    return lax.ppermute(value, "c", [(0, 1), (1, 0)])


def added(parts):
    return jnp.sum(parts.astype(jnp.float32), axis=0)


def own_units(proj_weight, proj_bias):
    units = jnp.concatenate(
        [
            proj_weight.reshape(ROWS * BLOCKS, 128),
            jnp.pad(proj_bias, (0, 128 - BIAS))[None],
            jnp.zeros((UNITS - ROWS * BLOCKS - 1, 128), jnp.bfloat16),
        ],
        axis=0,
    )
    mine = lax.axis_index("y") * X + lax.axis_index("x")
    return lax.dynamic_index_in_dim(units.reshape(HELP, PART, 128), mine, 0, keepdims=False)


def on_device(queries, key_rows, value_rows, grad_out, proj_weight, proj_bias, live_count):
    core = lax.axis_index("c").reshape(1)
    grads = grad_out.reshape(CAP * WIN, D)
    share = own_units(proj_weight, proj_bias)
    probs, attended, own, other = forward(live_count, core, queries, key_rows, value_rows, grads)
    both = added(jnp.stack([own, other_core(other)])).astype(jnp.bfloat16)
    over_help = exchange(both.reshape(HELP, PART, Z, 128), ("y", "x"))
    part = added(over_help).astype(jnp.bfloat16).transpose(1, 0, 2)
    shares = jnp.broadcast_to(share[None], (Z, PART, 128))
    over_z = exchange(jnp.concatenate([part, shares], axis=1), "z")
    whole = added(over_z[:, :PART])
    high = whole.astype(jnp.bfloat16)
    low = (whole - high.astype(jnp.float32)).astype(jnp.bfloat16)
    ends = jnp.pad(jnp.stack([high, low]), ((0, 0), (0, Z - PART), (0, 0)))
    sent = jnp.concatenate([over_z[:, PART:].transpose(1, 0, 2), ends], axis=0)
    near = exchange(jnp.broadcast_to(sent[None], (HELP, PART + 2, Z, 128)), ("y", "x"))
    encoded, grad_queries, grad_keys, grad_values = backward(
        live_count, core, queries, key_rows, value_rows, grads, probs, attended, near,
        other_core(near),
    )
    units = near[:, PART, :PART].astype(jnp.float32) + near[:, PART + 1, :PART].astype(jnp.float32)
    units = units.reshape(UNITS, 128)
    weight_grad = units[: ROWS * BLOCKS].reshape(ROWS, D)
    bias_grad = units[ROWS * BLOCKS, :BIAS]
    return (encoded, grad_queries, grad_keys, grad_values, weight_grad, bias_grad)


def solution(mesh):
    torus = Mesh(mesh.devices.reshape(Z, CORES, Y, X), ("z", "c", "y", "x"))
    windows = P(("z", "c", "y", "x"), None, None)
    lines, line = P(("z", "c"), None), P(("z", "c"))
    return jax.shard_map(
        on_device,
        mesh=torus,
        in_specs=(windows, windows, windows, windows, lines, line, P(("z", "c", "y", "x"))),
        out_specs=(windows, windows, windows, windows, lines, line),
        check_vma=False,
    )
```

```python
import jax
import jax.numpy as jnp
from jax import lax
from jax.experimental import pallas as pl
from jax.experimental.pallas import tpu as pltpu
from jax.sharding import Mesh
from jax.sharding import PartitionSpec as P

H = 8
HD = 80
WIN = 64
CAP = 5
ATTN = 640
D = 1280
Z, CORES, Y, X = 16, 2, 4, 4
SEQ = Z * CORES
HELP = Y * X
ROWS = ATTN // SEQ
BIAS = D // SEQ
BLOCKS = D // 128
PAIRS = H // 2
SPAN = 256
PART = 13
UNITS = HELP * PART
SCALE = HD**-0.5
VMEM_LIMIT = 24 * 1024 * 1024
NT = (((1,), (1,)), ((), ()))
TN = (((0,), (0,)), ((), ()))
NN = (((1,), (0,)), ((), ()))


def mm(left, right, dims):
    return lax.dot_general(left, right, dims, preferred_element_type=jnp.float32)


def head_masks(pair):
    lane = lax.broadcasted_iota(jnp.int32, (1, SPAN), 1)
    first = 32 * pair
    in_a = (lane >= first) & (lane < first + HD)
    in_b = (lane >= first + HD) & (lane < first + 2 * HD)
    return in_a.astype(jnp.float32), in_b.astype(jnp.float32)


def stacked(rows, mask_a, mask_b):
    return jnp.concatenate(
        [rows * mask_a.astype(jnp.bfloat16), rows * mask_b.astype(jnp.bfloat16)], axis=0
    )


def add_span(tiles, pair, value):
    for part in range(2):
        piece = value[:, 128 * part : 128 * (part + 1)]
        at = pair + part
        tiles[at] = piece if tiles[at] is None else tiles[at] + piece


def bias_pick():
    from_place = lax.broadcasted_iota(jnp.int32, (D, 128), 0)
    to_lane = lax.broadcasted_iota(jnp.int32, (D, 128), 1)
    owner = (from_place * 1639) >> 16
    return jnp.where(from_place - owner * BIAS == to_lane, 1.0, 0.0).astype(jnp.bfloat16)


def bias_owner(core):
    seq = lax.broadcasted_iota(jnp.int32, (Z, D), 0) * CORES + core
    place = lax.broadcasted_iota(jnp.int32, (Z, D), 1)
    return (place >= seq * BIAS) & (place < (seq + 1) * BIAS)


def row_order(my_core):
    place = lax.broadcasted_iota(jnp.int32, (1, ATTN), 1)
    half = jnp.where(place >= ATTN // 2, 1, 0)
    core = jnp.where(half == 0, my_core, 1 - my_core)
    inner = place - half * (ATTN // 2)
    feature = (inner & (Z - 1)) * (CORES * ROWS) + core * ROWS + (inner >> 4)
    rows = lax.broadcasted_iota(jnp.int32, (ATTN, ATTN), 0)
    return jnp.where(rows == feature, 1.0, 0.0).astype(jnp.bfloat16)


def forward_kernel(
    count_ref, core_ref, q_hbm, k_hbm, v_hbm, g_hbm, probs_ref, att_ref, own_ref, other_ref,
    q_ref, k_ref, v_ref, g_ref, natural, in_sems,
):
    count, my_core = count_ref[0], core_ref[0]
    moves = [
        pltpu.make_async_copy(there, here, in_sems.at[at])
        for at, (there, here) in enumerate(
            ((q_hbm, q_ref), (k_hbm, k_ref), (v_hbm, v_ref), (g_hbm, g_ref))
        )
    ]
    for move in moves:
        move.start()
    order = row_order(my_core)
    masks = [head_masks(pair) for pair in range(PAIRS)]
    for move in moves[:3]:
        move.wait()
    for w in range(CAP):
        rows = slice(WIN * w, WIN * (w + 1))
        tiles = [None] * (PAIRS + 1)
        for pair in range(PAIRS):
            span = slice(128 * pair, 128 * pair + SPAN)
            mask_a, mask_b = masks[pair]
            q_both = stacked(q_ref[w, :, span], mask_a, mask_b)
            scores = mm(k_ref[w, :, span], q_both, NT) * SCALE
            raised = jnp.exp(scores - jnp.max(scores, axis=0, keepdims=True))
            probs = raised * (1.0 / jnp.sum(raised, axis=0, keepdims=True))
            probs_ref[w, :, 128 * pair : 128 * (pair + 1)] = probs
            both = mm(probs.astype(jnp.bfloat16), v_ref[w, :, span], TN)
            add_span(tiles, pair, both[:WIN] * mask_a + both[WIN:] * mask_b)
        keep = jnp.where(w < count, 1.0, 0.0)
        for at, tile in enumerate(tiles):
            natural[rows, 128 * at : 128 * (at + 1)] = (tile * keep).astype(jnp.bfloat16)
    attended = mm(natural[...], order, NN).astype(jnp.bfloat16)
    att_ref[...] = attended
    row_of = lax.broadcasted_iota(jnp.int32, (16, CAP * WIN), 1)
    live_rows = jnp.where(row_of < count * WIN, 1.0, 0.0).astype(jnp.bfloat16)
    left = jnp.concatenate([attended.T, live_rows], axis=0)
    moves[3].wait()
    bias_parts = []
    for start in range(0, BLOCKS, 2):
        made = mm(left, g_ref[:, 128 * start : 128 * (start + 2)], NN)
        for block in range(2):
            cols = slice(128 * block, 128 * (block + 1))
            for row in range(ROWS):
                unit = row * BLOCKS + start + block
                own_ref[unit] = made[Z * row : Z * (row + 1), cols].astype(jnp.bfloat16)
                second = ATTN // 2 + Z * row
                other_ref[unit] = made[second : second + Z, cols].astype(jnp.bfloat16)
        bias_parts.append(made[ATTN : ATTN + 1])
    bias_row = jnp.concatenate(bias_parts, axis=1)
    pick = bias_pick()
    for core, wire_ref in ((my_core, own_ref), (1 - my_core, other_ref)):
        owned = jnp.where(bias_owner(core), jnp.broadcast_to(bias_row, (Z, D)), 0.0)
        wire_ref[ROWS * BLOCKS] = mm(owned.astype(jnp.bfloat16), pick, NN).astype(jnp.bfloat16)
        for unit in range(ROWS * BLOCKS + 1, UNITS):
            wire_ref[unit] = jnp.zeros((Z, 128), jnp.bfloat16)


def backward_kernel(
    count_ref, core_ref, q_hbm, k_hbm, v_hbm, g_hbm, probs_ref, att_ref, near_ref, far_ref,
    enc_hbm, dq_hbm, dk_hbm, dv_hbm,
    q_ref, k_ref, v_ref, g_ref, enc_ref, dq_ref, dk_ref, dv_ref,
    grad_att, weight_ref, in_sems, out_sems,
):
    count, my_core = count_ref[0], core_ref[0]
    moves = [
        pltpu.make_async_copy(there, here, in_sems.at[at])
        for at, (there, here) in enumerate(
            ((g_hbm, g_ref), (v_hbm, v_ref), (q_hbm, q_ref), (k_hbm, k_ref))
        )
    ]
    for move in moves:
        move.start()
    order = row_order(my_core)
    masks = [head_masks(pair) for pair in range(PAIRS)]
    bias_pieces = []
    for which, (held, core) in enumerate(((near_ref, my_core), (far_ref, 1 - my_core))):
        for unit in range(ROWS * BLOCKS + 1):
            owner, at = divmod(unit, PART)
            piece = held[owner, at]
            row, block = divmod(unit, BLOCKS)
            if row < ROWS:
                first = which * (ATTN // 2) + Z * row
                weight_ref[first : first + Z, 128 * block : 128 * (block + 1)] = piece
            else:
                spread = mm(piece, bias_pick(), NT)
                bias_pieces.append(jnp.where(bias_owner(core), spread, 0.0))
    bias = jnp.sum(bias_pieces[0] + bias_pieces[1], axis=0, keepdims=True)
    for move in moves:
        move.wait()
    ordered = mm(g_ref[...], weight_ref[...], NT).astype(jnp.bfloat16)
    grad_att[...] = mm(ordered, order, NT).astype(jnp.bfloat16)
    live_rows = lax.broadcasted_iota(jnp.int32, (CAP * WIN, 1), 0) < count * WIN
    for w in range(CAP):
        rows = slice(WIN * w, WIN * (w + 1))
        keep = jnp.where(w < count, 1.0, 0.0)
        dq_tiles, dk_tiles, dv_tiles = ([None] * (PAIRS + 1) for _ in range(3))
        for pair in range(PAIRS):
            span = slice(128 * pair, 128 * pair + SPAN)
            mask_a, mask_b = masks[pair]
            g_both = stacked(grad_att[rows, span], mask_a, mask_b)
            q_both = stacked(q_ref[w, :, span], mask_a, mask_b)
            grad_probs = mm(v_ref[w, :, span], g_both, NT)
            probs = probs_ref[w, :, 128 * pair : 128 * (pair + 1)]
            probs_low = probs.astype(jnp.bfloat16)
            delta = jnp.sum(probs_low.astype(jnp.float32) * grad_probs, axis=0, keepdims=True)
            grad_scores = (probs * (grad_probs - delta)).astype(jnp.bfloat16)
            add_span(dv_tiles, pair, mm(probs_low, g_both, NN))
            add_span(dk_tiles, pair, mm(grad_scores, q_both, NN))
            both = mm(grad_scores, k_ref[w, :, span], TN)
            add_span(dq_tiles, pair, both[:WIN] * mask_a + both[WIN:] * mask_b)
        for at in range(PAIRS + 1):
            cols = slice(128 * at, 128 * (at + 1))
            dq_ref[w, :, cols] = (dq_tiles[at] * (keep * SCALE)).astype(jnp.bfloat16)
            dk_ref[w, :, cols] = (dk_tiles[at] * (keep * SCALE)).astype(jnp.bfloat16)
            dv_ref[w, :, cols] = (dv_tiles[at] * keep).astype(jnp.bfloat16)
        cols = slice(256 * w, 256 * (w + 1))
        encoded = mm(att_ref[...], weight_ref[:, cols], NN) + bias[:, cols]
        encoded = jnp.where(live_rows, encoded, 0.0).astype(jnp.bfloat16)
        for window in range(CAP):
            enc_ref[window, :, cols] = encoded[WIN * window : WIN * (window + 1)]
    back = [
        pltpu.make_async_copy(made, out, out_sems.at[at])
        for at, (made, out) in enumerate(
            ((enc_ref, enc_hbm), (dq_ref, dq_hbm), (dk_ref, dk_hbm), (dv_ref, dv_hbm))
        )
    ]
    for move in back:
        move.start()
    for move in back:
        move.wait()


def in_hbm(value):
    return pltpu.with_memory_space_constraint(value, pltpu.HBM)


def in_vmem(value):
    return pltpu.with_memory_space_constraint(value, pltpu.VMEM)


def vmem_spec():
    return pl.BlockSpec(memory_space=pltpu.VMEM)


def hbm_spec():
    return pl.BlockSpec(memory_space=pltpu.HBM)


def smem_spec():
    return pl.BlockSpec(memory_space=pltpu.SMEM)


def forward(count, core, queries, key_rows, value_rows, grads):
    rows = pltpu.VMEM((CAP, WIN, ATTN), jnp.bfloat16)
    wire = pltpu.VMEM((UNITS, Z, 128), jnp.bfloat16)
    return pl.pallas_call(
        forward_kernel,
        out_shape=(
            pltpu.VMEM((CAP, WIN, H * WIN), jnp.float32),
            pltpu.VMEM((CAP * WIN, ATTN), jnp.bfloat16),
            wire,
            wire,
        ),
        in_specs=[smem_spec()] * 2 + [hbm_spec()] * 4,
        out_specs=(vmem_spec(),) * 4,
        scratch_shapes=[
            rows,
            rows,
            rows,
            pltpu.VMEM((CAP * WIN, D), jnp.bfloat16),
            pltpu.VMEM((CAP * WIN, ATTN), jnp.bfloat16),
            pltpu.SemaphoreType.DMA((4,)),
        ],
        compiler_params=pltpu.CompilerParams(vmem_limit_bytes=VMEM_LIMIT),
        cost_estimate=pl.CostEstimate(
            flops=1_000_000_000, bytes_accessed=5_000_000, transcendentals=200_000
        ),
    )(count, core, *(in_hbm(array) for array in (queries, key_rows, value_rows, grads)))


def backward(count, core, queries, key_rows, value_rows, grads, probs, attended, near, far):
    rows = jax.ShapeDtypeStruct((CAP, WIN, ATTN), jnp.bfloat16)
    held = pltpu.VMEM((CAP, WIN, ATTN), jnp.bfloat16)
    return pl.pallas_call(
        backward_kernel,
        out_shape=(jax.ShapeDtypeStruct((CAP, WIN, D), jnp.bfloat16), rows, rows, rows),
        in_specs=[smem_spec()] * 2 + [hbm_spec()] * 4 + [vmem_spec()] * 4,
        out_specs=(hbm_spec(),) * 4,
        scratch_shapes=[
            held,
            held,
            held,
            pltpu.VMEM((CAP * WIN, D), jnp.bfloat16),
            pltpu.VMEM((CAP, WIN, D), jnp.bfloat16),
            held,
            held,
            held,
            pltpu.VMEM((CAP * WIN, ATTN), jnp.bfloat16),
            pltpu.VMEM((ATTN, D), jnp.bfloat16),
            pltpu.SemaphoreType.DMA((4,)),
            pltpu.SemaphoreType.DMA((4,)),
        ],
        compiler_params=pltpu.CompilerParams(vmem_limit_bytes=VMEM_LIMIT),
        cost_estimate=pl.CostEstimate(
            flops=1_700_000_000, bytes_accessed=8_000_000, transcendentals=0
        ),
    )(
        count, core, *(in_hbm(array) for array in (queries, key_rows, value_rows, grads)),
        *(in_vmem(array) for array in (probs, attended, near, far)),
    )


def exchange(blocks, axis):
    return lax.all_to_all(blocks, axis, 0, 0, tiled=True)


def other_core(value):
    return lax.ppermute(value, "c", [(0, 1), (1, 0)])


def added(parts):
    return jnp.sum(parts.astype(jnp.float32), axis=0)


def own_units(proj_weight, proj_bias):
    units = jnp.concatenate(
        [
            proj_weight.reshape(ROWS * BLOCKS, 128),
            jnp.pad(proj_bias, (0, 128 - BIAS))[None],
            jnp.zeros((UNITS - ROWS * BLOCKS - 1, 128), jnp.bfloat16),
        ],
        axis=0,
    )
    mine = lax.axis_index("y") * X + lax.axis_index("x")
    return lax.dynamic_index_in_dim(units.reshape(HELP, PART, 128), mine, 0, keepdims=False)


def on_device(queries, key_rows, value_rows, grad_out, proj_weight, proj_bias, live_count):
    core = lax.axis_index("c").reshape(1)
    grads = grad_out.reshape(CAP * WIN, D)
    share = own_units(proj_weight, proj_bias)
    probs, attended, own, other = forward(live_count, core, queries, key_rows, value_rows, grads)
    both = added(jnp.stack([own, other_core(other)])).astype(jnp.bfloat16)
    over_help = exchange(both.reshape(HELP, PART, Z, 128), ("y", "x"))
    part = added(over_help).astype(jnp.bfloat16).transpose(1, 0, 2)
    shares = jnp.broadcast_to(share[None], (Z, PART, 128))
    over_z = exchange(jnp.concatenate([part, shares], axis=1), "z")
    whole = added(over_z[:, :PART])
    high = whole.astype(jnp.bfloat16)
    low = (whole - high.astype(jnp.float32)).astype(jnp.bfloat16)
    ends = jnp.pad(jnp.stack([high, low]), ((0, 0), (0, Z - PART), (0, 0)))
    sent = jnp.concatenate([over_z[:, PART:].transpose(1, 0, 2), ends], axis=0)
    near = exchange(jnp.broadcast_to(sent[None], (HELP, PART + 2, Z, 128)), ("y", "x"))
    encoded, grad_queries, grad_keys, grad_values = backward(
        live_count, core, queries, key_rows, value_rows, grads, probs, attended, near,
        other_core(near),
    )
    units = near[:, PART, :PART].astype(jnp.float32) + near[:, PART + 1, :PART].astype(jnp.float32)
    units = units.reshape(UNITS, 128)
    weight_grad = units[: ROWS * BLOCKS].reshape(ROWS, D)
    bias_grad = units[ROWS * BLOCKS, :BIAS]
    return (encoded, grad_queries, grad_keys, grad_values, weight_grad, bias_grad)


def solution(mesh):
    torus = Mesh(mesh.devices.reshape(Z, CORES, Y, X), ("z", "c", "y", "x"))
    windows = P(("z", "c", "y", "x"), None, None)
    lines, line = P(("z", "c"), None), P(("z", "c"))
    return jax.shard_map(
        on_device,
        mesh=torus,
        in_specs=(windows, windows, windows, windows, lines, line, P(("z", "c", "y", "x"))),
        out_specs=(windows, windows, windows, windows, lines, line),
        check_vma=False,
    )
```

```python
import jax
import jax.numpy as jnp
from jax import lax
from jax.experimental import pallas as pl
from jax.experimental.pallas import tpu as pltpu
from jax.sharding import Mesh
from jax.sharding import PartitionSpec as P

H = 8
HD = 80
WIN = 64
CAP = 5
ATTN = 640
D = 1280
Z, CORES, Y, X = 16, 2, 4, 4
SEQ = Z * CORES
HELP = Y * X
ROWS = ATTN // SEQ
BIAS = D // SEQ
HALF = ATTN // 2
BLOCKS = D // 128
PAIRS = H // 2
SPAN = 256
PART = 13
UNITS = HELP * PART
SCALE = HD**-0.5
VMEM_LIMIT = 24 * 1024 * 1024
NT = (((1,), (1,)), ((), ()))
TN = (((0,), (0,)), ((), ()))
NN = (((1,), (0,)), ((), ()))


def mm(left, right, dims):
    return lax.dot_general(left, right, dims, preferred_element_type=jnp.float32)


def head_masks(pair):
    lane = lax.broadcasted_iota(jnp.int32, (1, SPAN), 1)
    first = 32 * pair
    in_a = (lane >= first) & (lane < first + HD)
    in_b = (lane >= first + HD) & (lane < first + 2 * HD)
    return in_a.astype(jnp.float32), in_b.astype(jnp.float32)


def stacked(rows, mask_a, mask_b):
    return jnp.concatenate(
        [rows * mask_a.astype(jnp.bfloat16), rows * mask_b.astype(jnp.bfloat16)], axis=0
    )


def add_span(tiles, pair, value):
    for part in range(2):
        piece = value[:, 128 * part : 128 * (part + 1)]
        at = pair + part
        tiles[at] = piece if tiles[at] is None else tiles[at] + piece


def bias_pick():
    from_place = lax.broadcasted_iota(jnp.int32, (D, 128), 0)
    to_lane = lax.broadcasted_iota(jnp.int32, (D, 128), 1)
    owner = (from_place * 1639) >> 16
    return jnp.where(from_place - owner * BIAS == to_lane, 1.0, 0.0).astype(jnp.bfloat16)


def bias_owner(core):
    seq = lax.broadcasted_iota(jnp.int32, (Z, D), 0) * CORES + core
    place = lax.broadcasted_iota(jnp.int32, (Z, D), 1)
    return (place >= seq * BIAS) & (place < (seq + 1) * BIAS)


def row_order(core):
    place = lax.broadcasted_iota(jnp.int32, (1, HALF), 1)
    feature = (place & (Z - 1)) * (CORES * ROWS) + core * ROWS + (place >> 4)
    rows = lax.broadcasted_iota(jnp.int32, (ATTN, HALF), 0)
    return jnp.where(rows == feature, 1.0, 0.0).astype(jnp.bfloat16)


def copies(pairs, sems):
    return [
        pltpu.make_async_copy(there, here, sems.at[at]) for at, (there, here) in enumerate(pairs)
    ]


def put_units(wire_ref, made, start):
    for block in range(2):
        for row in range(ROWS):
            wire_ref[row * BLOCKS + start + block] = made[
                Z * row : Z * (row + 1), 128 * block : 128 * (block + 1)
            ].astype(jnp.bfloat16)


def put_bias(wire_ref, bias_row, core):
    owned = jnp.where(bias_owner(core), jnp.broadcast_to(bias_row, (Z, D)), 0.0)
    wire_ref[ROWS * BLOCKS] = mm(owned.astype(jnp.bfloat16), bias_pick(), NN).astype(jnp.bfloat16)
    for unit in range(ROWS * BLOCKS + 1, UNITS):
        wire_ref[unit] = jnp.zeros((Z, 128), jnp.bfloat16)


def take_units(held, weight_ref, core):
    for unit in range(ROWS * BLOCKS):
        owner, at = divmod(unit, PART)
        row, block = divmod(unit, BLOCKS)
        weight_ref[Z * row : Z * (row + 1), 128 * block : 128 * (block + 1)] = held[owner, at]
    owner, at = divmod(ROWS * BLOCKS, PART)
    spread = mm(held[owner, at], bias_pick(), NT)
    return jnp.sum(jnp.where(bias_owner(core), spread, 0.0), axis=0, keepdims=True)


def forward_kernel(
    count_ref, core_ref, q_hbm, k_hbm, v_hbm, g_hbm,
    probs_ref, att_own_ref, att_other_ref, left_ref, g_ref, bias_ref, other_ref,
    q_ref, k_ref, v_ref, natural, in_sems,
):
    count, my_core = count_ref[0], core_ref[0]
    moves = copies(((q_hbm, q_ref), (k_hbm, k_ref), (v_hbm, v_ref), (g_hbm, g_ref)), in_sems)
    for move in moves:
        move.start()
    order_own, order_other = row_order(my_core), row_order(1 - my_core)
    masks = [head_masks(pair) for pair in range(PAIRS)]
    for move in moves[:3]:
        move.wait()
    for w in range(CAP):
        rows = slice(WIN * w, WIN * (w + 1))
        tiles = [None] * (PAIRS + 1)
        for pair in range(PAIRS):
            span = slice(128 * pair, 128 * pair + SPAN)
            mask_a, mask_b = masks[pair]
            q_both = stacked(q_ref[w, :, span], mask_a, mask_b)
            scores = mm(k_ref[w, :, span], q_both, NT) * SCALE
            raised = jnp.exp(scores - jnp.max(scores, axis=0, keepdims=True))
            probs = raised * (1.0 / jnp.sum(raised, axis=0, keepdims=True))
            probs_ref[w, :, 128 * pair : 128 * (pair + 1)] = probs
            both = mm(probs.astype(jnp.bfloat16), v_ref[w, :, span], TN)
            add_span(tiles, pair, both[:WIN] * mask_a + both[WIN:] * mask_b)
        keep = jnp.where(w < count, 1.0, 0.0)
        for at, tile in enumerate(tiles):
            natural[rows, 128 * at : 128 * (at + 1)] = (tile * keep).astype(jnp.bfloat16)
    att_other = mm(natural[...], order_other, NN).astype(jnp.bfloat16)
    att_other_ref[...] = att_other
    att_own = mm(natural[...], order_own, NN).astype(jnp.bfloat16)
    att_own_ref[...] = att_own
    left_ref[...] = att_own.T
    row_of = lax.broadcasted_iota(jnp.int32, (16, CAP * WIN), 1)
    live_rows = jnp.where(row_of < count * WIN, 1.0, 0.0).astype(jnp.bfloat16)
    left = jnp.concatenate([att_other.T, live_rows], axis=0)
    moves[3].wait()
    bias_parts = []
    for start in range(0, BLOCKS, 2):
        made = mm(left, g_ref[:, 128 * start : 128 * (start + 2)], NN)
        put_units(other_ref, made, start)
        bias_parts.append(made[HALF : HALF + 1])
    bias_row = jnp.concatenate(bias_parts, axis=1)
    bias_ref[...] = bias_row
    put_bias(other_ref, bias_row, 1 - my_core)


def own_kernel(core_ref, left_ref, g_ref, bias_ref, own_ref):
    for start in range(0, BLOCKS, 2):
        put_units(own_ref, mm(left_ref[...], g_ref[:, 128 * start : 128 * (start + 2)], NN), start)
    put_bias(own_ref, bias_ref[...], core_ref[0])


def near_kernel(
    core_ref, q_hbm, k_hbm, v_hbm, g_hbm, att_own_ref, near_ref,
    q_ref, k_ref, v_ref, g_ref, first_ref, sum_ref, weight_ref, in_sems,
):
    moves = copies(((g_hbm, g_ref), (v_hbm, v_ref), (q_hbm, q_ref), (k_hbm, k_ref)), in_sems)
    for move in moves:
        move.start()
    bias = take_units(near_ref, weight_ref, core_ref[0])
    for start in range(0, D, SPAN):
        cols = slice(start, start + SPAN)
        sum_ref[:, cols] = mm(att_own_ref[...], weight_ref[:, cols], NN) + bias[:, cols]
    moves[0].wait()
    first_ref[...] = mm(g_ref[...], weight_ref[...], NT).astype(jnp.bfloat16)
    for move in moves[1:]:
        move.wait()


def backward_kernel(
    count_ref, core_ref, q_ref, k_ref, v_ref, g_ref, probs_ref, att_ref, first_ref, sum_ref,
    far_ref, enc_hbm, dq_hbm, dk_hbm, dv_hbm,
    enc_ref, dq_ref, dk_ref, dv_ref, grad_att, weight_ref, out_sems,
):
    count, my_core = count_ref[0], core_ref[0]
    masks = [head_masks(pair) for pair in range(PAIRS)]
    bias = take_units(far_ref, weight_ref, 1 - my_core)
    second = mm(g_ref[...], weight_ref[...], NT).astype(jnp.bfloat16)
    grad_att[...] = (
        mm(first_ref[...], row_order(my_core), NT) + mm(second, row_order(1 - my_core), NT)
    ).astype(jnp.bfloat16)
    live_rows = lax.broadcasted_iota(jnp.int32, (CAP * WIN, 1), 0) < count * WIN
    for w in range(CAP):
        rows = slice(WIN * w, WIN * (w + 1))
        keep = jnp.where(w < count, 1.0, 0.0)
        dq_tiles, dk_tiles, dv_tiles = ([None] * (PAIRS + 1) for _ in range(3))
        for pair in range(PAIRS):
            span = slice(128 * pair, 128 * pair + SPAN)
            mask_a, mask_b = masks[pair]
            g_both = stacked(grad_att[rows, span], mask_a, mask_b)
            q_both = stacked(q_ref[w, :, span], mask_a, mask_b)
            grad_probs = mm(v_ref[w, :, span], g_both, NT)
            probs = probs_ref[w, :, 128 * pair : 128 * (pair + 1)]
            probs_low = probs.astype(jnp.bfloat16)
            delta = jnp.sum(probs_low.astype(jnp.float32) * grad_probs, axis=0, keepdims=True)
            grad_scores = (probs * (grad_probs - delta)).astype(jnp.bfloat16)
            add_span(dv_tiles, pair, mm(probs_low, g_both, NN))
            add_span(dk_tiles, pair, mm(grad_scores, q_both, NN))
            both = mm(grad_scores, k_ref[w, :, span], TN)
            add_span(dq_tiles, pair, both[:WIN] * mask_a + both[WIN:] * mask_b)
        for at in range(PAIRS + 1):
            cols = slice(128 * at, 128 * (at + 1))
            dq_ref[w, :, cols] = (dq_tiles[at] * (keep * SCALE)).astype(jnp.bfloat16)
            dk_ref[w, :, cols] = (dk_tiles[at] * (keep * SCALE)).astype(jnp.bfloat16)
            dv_ref[w, :, cols] = (dv_tiles[at] * keep).astype(jnp.bfloat16)
        cols = slice(SPAN * w, SPAN * (w + 1))
        encoded = sum_ref[:, cols] + mm(att_ref[...], weight_ref[:, cols], NN) + bias[:, cols]
        encoded = jnp.where(live_rows, encoded, 0.0).astype(jnp.bfloat16)
        for window in range(CAP):
            enc_ref[window, :, cols] = encoded[WIN * window : WIN * (window + 1)]
    back = copies(
        ((enc_ref, enc_hbm), (dq_ref, dq_hbm), (dk_ref, dk_hbm), (dv_ref, dv_hbm)), out_sems
    )
    for move in back:
        move.start()
    for move in back:
        move.wait()


def in_hbm(value):
    return pltpu.with_memory_space_constraint(value, pltpu.HBM)


def in_vmem(value):
    return pltpu.with_memory_space_constraint(value, pltpu.VMEM)


def vmem_spec():
    return pl.BlockSpec(memory_space=pltpu.VMEM)


def hbm_spec():
    return pl.BlockSpec(memory_space=pltpu.HBM)


def smem_spec():
    return pl.BlockSpec(memory_space=pltpu.SMEM)


def call(kernel, out_shape, in_specs, out_spec, scratch_shapes, flops):
    return pl.pallas_call(
        kernel,
        out_shape=out_shape,
        in_specs=in_specs,
        out_specs=(out_spec,) * len(out_shape),
        scratch_shapes=scratch_shapes,
        compiler_params=pltpu.CompilerParams(vmem_limit_bytes=VMEM_LIMIT),
        cost_estimate=pl.CostEstimate(flops=flops, bytes_accessed=4_000_000, transcendentals=0),
    )


def forward(count, core, queries, key_rows, value_rows, grads):
    rows = pltpu.VMEM((CAP, WIN, ATTN), jnp.bfloat16)
    half = pltpu.VMEM((CAP * WIN, HALF), jnp.bfloat16)
    return call(
        forward_kernel,
        (
            pltpu.VMEM((CAP, WIN, H * WIN), jnp.float32),
            half,
            half,
            pltpu.VMEM((HALF, CAP * WIN), jnp.bfloat16),
            pltpu.VMEM((CAP * WIN, D), jnp.bfloat16),
            pltpu.VMEM((1, D), jnp.float32),
            pltpu.VMEM((UNITS, Z, 128), jnp.bfloat16),
        ),
        [smem_spec()] * 2 + [hbm_spec()] * 4,
        vmem_spec(),
        [
            rows, rows, rows, pltpu.VMEM((CAP * WIN, ATTN), jnp.bfloat16),
            pltpu.SemaphoreType.DMA((4,)),
        ],
        800_000_000,
    )(count, core, *(in_hbm(array) for array in (queries, key_rows, value_rows, grads)))


def own_half(core, left, grads, bias_row):
    return call(
        own_kernel,
        (pltpu.VMEM((UNITS, Z, 128), jnp.bfloat16),),
        [smem_spec()] + [vmem_spec()] * 3,
        vmem_spec(),
        [],
        300_000_000,
    )(core, *(in_vmem(array) for array in (left, grads, bias_row)))[0]


def near_half(core, queries, key_rows, value_rows, grads, att_own, near):
    rows = pltpu.VMEM((CAP, WIN, ATTN), jnp.bfloat16)
    return call(
        near_kernel,
        (
            rows, rows, rows, pltpu.VMEM((CAP * WIN, D), jnp.bfloat16),
            pltpu.VMEM((CAP * WIN, HALF), jnp.bfloat16), pltpu.VMEM((CAP * WIN, D), jnp.float32),
        ),
        [smem_spec()] + [hbm_spec()] * 4 + [vmem_spec()] * 2,
        vmem_spec(),
        [pltpu.VMEM((HALF, D), jnp.bfloat16), pltpu.SemaphoreType.DMA((4,))],
        600_000_000,
    )(
        core, *(in_hbm(array) for array in (queries, key_rows, value_rows, grads)),
        in_vmem(att_own), in_vmem(near),
    )


def backward(count, core, *held):
    rows = jax.ShapeDtypeStruct((CAP, WIN, ATTN), jnp.bfloat16)
    made = pltpu.VMEM((CAP, WIN, ATTN), jnp.bfloat16)
    return call(
        backward_kernel,
        (jax.ShapeDtypeStruct((CAP, WIN, D), jnp.bfloat16), rows, rows, rows),
        [smem_spec()] * 2 + [vmem_spec()] * 9,
        hbm_spec(),
        [
            pltpu.VMEM((CAP, WIN, D), jnp.bfloat16), made, made, made,
            pltpu.VMEM((CAP * WIN, ATTN), jnp.bfloat16), pltpu.VMEM((HALF, D), jnp.bfloat16),
            pltpu.SemaphoreType.DMA((4,)),
        ],
        1_200_000_000,
    )(count, core, *(in_vmem(array) for array in held))


def exchange(blocks, axis):
    return lax.all_to_all(blocks, axis, 0, 0, tiled=True)


def other_core(value):
    return lax.ppermute(value, "c", [(0, 1), (1, 0)])


def added(parts):
    return jnp.sum(parts.astype(jnp.float32), axis=0)


def own_units(proj_weight, proj_bias):
    units = jnp.concatenate(
        [
            proj_weight.reshape(ROWS * BLOCKS, 128),
            jnp.pad(proj_bias, (0, 128 - BIAS))[None],
            jnp.zeros((UNITS - ROWS * BLOCKS - 1, 128), jnp.bfloat16),
        ],
        axis=0,
    )
    mine = lax.axis_index("y") * X + lax.axis_index("x")
    return lax.dynamic_index_in_dim(units.reshape(HELP, PART, 128), mine, 0, keepdims=False)


def on_device(queries, key_rows, value_rows, grad_out, proj_weight, proj_bias, live_count):
    core = lax.axis_index("c").reshape(1)
    grads = grad_out.reshape(CAP * WIN, D)
    share = own_units(proj_weight, proj_bias)
    probs, att_own, att_other, left, held_grads, bias_row, other = forward(
        live_count, core, queries, key_rows, value_rows, grads
    )
    own = own_half(core, left, held_grads, bias_row)
    both = added(jnp.stack([own, other_core(other)])).astype(jnp.bfloat16)
    over_help = exchange(both.reshape(HELP, PART, Z, 128), ("y", "x"))
    part = added(over_help).astype(jnp.bfloat16).transpose(1, 0, 2)
    shares = jnp.broadcast_to(share[None], (Z, PART, 128))
    over_z = exchange(jnp.concatenate([part, shares], axis=1), "z")
    whole = added(over_z[:, :PART])
    high = whole.astype(jnp.bfloat16)
    low = (whole - high.astype(jnp.float32)).astype(jnp.bfloat16)
    ends = jnp.pad(jnp.stack([high, low]), ((0, 0), (0, Z - PART), (0, 0)))
    sent = jnp.concatenate([over_z[:, PART:].transpose(1, 0, 2), ends], axis=0)
    near = exchange(jnp.broadcast_to(sent[None], (HELP, PART + 2, Z, 128)), ("y", "x"))
    *held, first, partial = near_half(core, queries, key_rows, value_rows, grads, att_own, near)
    encoded, grad_queries, grad_keys, grad_values = backward(
        live_count, core, *held, probs, att_other, first, partial, other_core(near)
    )
    units = near[:, PART, :PART].astype(jnp.float32) + near[:, PART + 1, :PART].astype(jnp.float32)
    units = units.reshape(UNITS, 128)
    weight_grad = units[: ROWS * BLOCKS].reshape(ROWS, D)
    bias_grad = units[ROWS * BLOCKS, :BIAS]
    return (encoded, grad_queries, grad_keys, grad_values, weight_grad, bias_grad)


def solution(mesh):
    torus = Mesh(mesh.devices.reshape(Z, CORES, Y, X), ("z", "c", "y", "x"))
    windows = P(("z", "c", "y", "x"), None, None)
    lines, line = P(("z", "c"), None), P(("z", "c"))
    return jax.shard_map(
        on_device,
        mesh=torus,
        in_specs=(windows, windows, windows, windows, lines, line, P(("z", "c", "y", "x"))),
        out_specs=(windows, windows, windows, windows, lines, line),
        check_vma=False,
    )
```

```python
import jax
import jax.numpy as jnp
from jax import lax
from jax.experimental import pallas as pl
from jax.experimental.pallas import tpu as pltpu
from jax.sharding import Mesh
from jax.sharding import PartitionSpec as P

H = 8
HD = 80
WIN = 64
CAP = 5
ATTN = 640
D = 1280
Z, CORES, Y, X = 16, 2, 4, 4
SEQ = Z * CORES
HELP = Y * X
ROWS = ATTN // SEQ
BIAS = D // SEQ
HALF = ATTN // 2
BLOCKS = D // 128
PAIRS = H // 2
SPAN = 256
PART = 13
UNITS = HELP * PART
SCALE = HD**-0.5
VMEM_LIMIT = 24 * 1024 * 1024
NT = (((1,), (1,)), ((), ()))
TN = (((0,), (0,)), ((), ()))
NN = (((1,), (0,)), ((), ()))


def mm(left, right, dims):
    return lax.dot_general(left, right, dims, preferred_element_type=jnp.float32)


def head_masks(pair):
    lane = lax.broadcasted_iota(jnp.int32, (1, SPAN), 1)
    first = 32 * pair
    in_a = (lane >= first) & (lane < first + HD)
    in_b = (lane >= first + HD) & (lane < first + 2 * HD)
    return in_a.astype(jnp.float32), in_b.astype(jnp.float32)


def stacked(rows, mask_a, mask_b):
    return jnp.concatenate(
        [rows * mask_a.astype(jnp.bfloat16), rows * mask_b.astype(jnp.bfloat16)], axis=0
    )


def add_span(tiles, pair, value):
    for part in range(2):
        piece = value[:, 128 * part : 128 * (part + 1)]
        at = pair + part
        tiles[at] = piece if tiles[at] is None else tiles[at] + piece


def bias_pick():
    from_place = lax.broadcasted_iota(jnp.int32, (D, 128), 0)
    to_lane = lax.broadcasted_iota(jnp.int32, (D, 128), 1)
    owner = (from_place * 1639) >> 16
    return jnp.where(from_place - owner * BIAS == to_lane, 1.0, 0.0).astype(jnp.bfloat16)


def bias_owner(core):
    seq = lax.broadcasted_iota(jnp.int32, (Z, D), 0) * CORES + core
    place = lax.broadcasted_iota(jnp.int32, (Z, D), 1)
    return (place >= seq * BIAS) & (place < (seq + 1) * BIAS)


def row_order(core):
    place = lax.broadcasted_iota(jnp.int32, (1, HALF), 1)
    feature = (place & (Z - 1)) * (CORES * ROWS) + core * ROWS + (place >> 4)
    rows = lax.broadcasted_iota(jnp.int32, (ATTN, HALF), 0)
    return jnp.where(rows == feature, 1.0, 0.0).astype(jnp.bfloat16)


def copies(pairs, sems):
    return [
        pltpu.make_async_copy(there, here, sems.at[at]) for at, (there, here) in enumerate(pairs)
    ]


def put_units(wire_ref, made, start):
    for block in range(2):
        for row in range(ROWS):
            wire_ref[row * BLOCKS + start + block] = made[
                Z * row : Z * (row + 1), 128 * block : 128 * (block + 1)
            ].astype(jnp.bfloat16)


def put_bias(wire_ref, bias_row, core):
    owned = jnp.where(bias_owner(core), jnp.broadcast_to(bias_row, (Z, D)), 0.0)
    wire_ref[ROWS * BLOCKS] = mm(owned.astype(jnp.bfloat16), bias_pick(), NN).astype(jnp.bfloat16)
    for unit in range(ROWS * BLOCKS + 1, UNITS):
        wire_ref[unit] = jnp.zeros((Z, 128), jnp.bfloat16)


def take_units(held, weight_ref, core):
    for unit in range(ROWS * BLOCKS):
        owner, at = divmod(unit, PART)
        row, block = divmod(unit, BLOCKS)
        weight_ref[Z * row : Z * (row + 1), 128 * block : 128 * (block + 1)] = held[owner, at]
    owner, at = divmod(ROWS * BLOCKS, PART)
    spread = mm(held[owner, at], bias_pick(), NT)
    return jnp.sum(jnp.where(bias_owner(core), spread, 0.0), axis=0, keepdims=True)


def forward_kernel(
    count_ref, core_ref, q_hbm, k_hbm, v_hbm, g_hbm,
    probs_ref, natural, att_other_ref, g_ref, bias_ref, other_ref,
    q_ref, k_ref, v_ref, in_sems,
):
    count, my_core = count_ref[0], core_ref[0]
    moves = copies(((q_hbm, q_ref), (k_hbm, k_ref), (v_hbm, v_ref), (g_hbm, g_ref)), in_sems)
    for move in moves:
        move.start()
    order_other = row_order(1 - my_core)
    masks = [head_masks(pair) for pair in range(PAIRS)]
    for move in moves[:3]:
        move.wait()
    for w in range(CAP):
        rows = slice(WIN * w, WIN * (w + 1))
        tiles = [None] * (PAIRS + 1)
        for pair in range(PAIRS):
            span = slice(128 * pair, 128 * pair + SPAN)
            mask_a, mask_b = masks[pair]
            q_both = stacked(q_ref[w, :, span], mask_a, mask_b)
            scores = mm(k_ref[w, :, span], q_both, NT) * SCALE
            raised = jnp.exp(scores - jnp.max(scores, axis=0, keepdims=True))
            probs = raised * (1.0 / jnp.sum(raised, axis=0, keepdims=True))
            probs_ref[w, :, 128 * pair : 128 * (pair + 1)] = probs
            both = mm(probs.astype(jnp.bfloat16), v_ref[w, :, span], TN)
            add_span(tiles, pair, both[:WIN] * mask_a + both[WIN:] * mask_b)
        keep = jnp.where(w < count, 1.0, 0.0)
        for at, tile in enumerate(tiles):
            natural[rows, 128 * at : 128 * (at + 1)] = (tile * keep).astype(jnp.bfloat16)
    att_other = mm(natural[...], order_other, NN).astype(jnp.bfloat16)
    att_other_ref[...] = att_other
    row_of = lax.broadcasted_iota(jnp.int32, (16, CAP * WIN), 1)
    live_rows = jnp.where(row_of < count * WIN, 1.0, 0.0).astype(jnp.bfloat16)
    left = jnp.concatenate([att_other.T, live_rows], axis=0)
    moves[3].wait()
    bias_parts = []
    for start in range(0, BLOCKS, 2):
        made = mm(left, g_ref[:, 128 * start : 128 * (start + 2)], NN)
        put_units(other_ref, made, start)
        bias_parts.append(made[HALF : HALF + 1])
    bias_row = jnp.concatenate(bias_parts, axis=1)
    bias_ref[...] = bias_row
    put_bias(other_ref, bias_row, 1 - my_core)


def own_kernel(core_ref, natural, g_ref, bias_ref, own_ref, att_own_ref):
    att_own = mm(natural[...], row_order(core_ref[0]), NN).astype(jnp.bfloat16)
    att_own_ref[...] = att_own
    left = att_own.T
    for start in range(0, BLOCKS, 2):
        put_units(own_ref, mm(left, g_ref[:, 128 * start : 128 * (start + 2)], NN), start)
    put_bias(own_ref, bias_ref[...], core_ref[0])


def near_kernel(
    core_ref, q_hbm, k_hbm, v_hbm, g_hbm, att_own_ref, near_ref,
    q_ref, k_ref, v_ref, g_ref, first_ref, sum_ref, grad_hbm, weight_ref, grad_ref, in_sems,
    out_sem,
):
    moves = copies(((g_hbm, g_ref), (v_hbm, v_ref), (q_hbm, q_ref), (k_hbm, k_ref)), in_sems)
    for move in moves:
        move.start()
    for owner in range(HELP):
        made = near_ref[owner, PART].astype(jnp.float32)
        for at in range(PART):
            row, block = divmod(owner * PART + at, BLOCKS)
            if row < ROWS:
                grad_ref[row : row + 1, 128 * block : 128 * (block + 1)] = made[at : at + 1]
    grad_move = pltpu.make_async_copy(grad_ref, grad_hbm, out_sem)
    grad_move.start()
    bias = take_units(near_ref, weight_ref, core_ref[0])
    for start in range(0, D, SPAN):
        cols = slice(start, start + SPAN)
        sum_ref[:, cols] = mm(att_own_ref[...], weight_ref[:, cols], NN) + bias[:, cols]
    moves[0].wait()
    first_ref[...] = mm(g_ref[...], weight_ref[...], NT).astype(jnp.bfloat16)
    for move in moves[1:]:
        move.wait()
    grad_move.wait()


def backward_kernel(
    count_ref, core_ref, q_ref, k_ref, v_ref, g_ref, probs_ref, att_ref, first_ref, sum_ref,
    far_ref, enc_hbm, dq_hbm, dk_hbm, dv_hbm,
    enc_ref, dq_ref, dk_ref, dv_ref, grad_att, weight_ref, out_sems,
):
    count, my_core = count_ref[0], core_ref[0]
    masks = [head_masks(pair) for pair in range(PAIRS)]
    bias = take_units(far_ref, weight_ref, 1 - my_core)
    second = mm(g_ref[...], weight_ref[...], NT).astype(jnp.bfloat16)
    grad_att[...] = (
        mm(first_ref[...], row_order(my_core), NT) + mm(second, row_order(1 - my_core), NT)
    ).astype(jnp.bfloat16)
    live_rows = lax.broadcasted_iota(jnp.int32, (CAP * WIN, 1), 0) < count * WIN
    for w in range(CAP):
        rows = slice(WIN * w, WIN * (w + 1))
        keep = jnp.where(w < count, 1.0, 0.0)
        dq_tiles, dk_tiles, dv_tiles = ([None] * (PAIRS + 1) for _ in range(3))
        for pair in range(PAIRS):
            span = slice(128 * pair, 128 * pair + SPAN)
            mask_a, mask_b = masks[pair]
            g_both = stacked(grad_att[rows, span], mask_a, mask_b)
            q_both = stacked(q_ref[w, :, span], mask_a, mask_b)
            grad_probs = mm(v_ref[w, :, span], g_both, NT)
            probs = probs_ref[w, :, 128 * pair : 128 * (pair + 1)]
            probs_low = probs.astype(jnp.bfloat16)
            delta = jnp.sum(probs_low.astype(jnp.float32) * grad_probs, axis=0, keepdims=True)
            grad_scores = (probs * (grad_probs - delta)).astype(jnp.bfloat16)
            add_span(dv_tiles, pair, mm(probs_low, g_both, NN))
            add_span(dk_tiles, pair, mm(grad_scores, q_both, NN))
            both = mm(grad_scores, k_ref[w, :, span], TN)
            add_span(dq_tiles, pair, both[:WIN] * mask_a + both[WIN:] * mask_b)
        for at in range(PAIRS + 1):
            cols = slice(128 * at, 128 * (at + 1))
            dq_ref[w, :, cols] = (dq_tiles[at] * (keep * SCALE)).astype(jnp.bfloat16)
            dk_ref[w, :, cols] = (dk_tiles[at] * (keep * SCALE)).astype(jnp.bfloat16)
            dv_ref[w, :, cols] = (dv_tiles[at] * keep).astype(jnp.bfloat16)
        cols = slice(SPAN * w, SPAN * (w + 1))
        encoded = sum_ref[:, cols] + mm(att_ref[...], weight_ref[:, cols], NN) + bias[:, cols]
        encoded = jnp.where(live_rows, encoded, 0.0).astype(jnp.bfloat16)
        for window in range(CAP):
            enc_ref[window, :, cols] = encoded[WIN * window : WIN * (window + 1)]
    back = copies(
        ((enc_ref, enc_hbm), (dq_ref, dq_hbm), (dk_ref, dk_hbm), (dv_ref, dv_hbm)), out_sems
    )
    for move in back:
        move.start()
    for move in back:
        move.wait()


def in_hbm(value):
    return pltpu.with_memory_space_constraint(value, pltpu.HBM)


def in_vmem(value):
    return pltpu.with_memory_space_constraint(value, pltpu.VMEM)


def vmem_spec():
    return pl.BlockSpec(memory_space=pltpu.VMEM)


def hbm_spec():
    return pl.BlockSpec(memory_space=pltpu.HBM)


def smem_spec():
    return pl.BlockSpec(memory_space=pltpu.SMEM)


def call(kernel, out_shape, in_specs, out_specs, scratch_shapes, flops):
    return pl.pallas_call(
        kernel,
        out_shape=out_shape,
        in_specs=in_specs,
        out_specs=out_specs,
        scratch_shapes=scratch_shapes,
        compiler_params=pltpu.CompilerParams(vmem_limit_bytes=VMEM_LIMIT),
        cost_estimate=pl.CostEstimate(flops=flops, bytes_accessed=4_000_000, transcendentals=0),
    )


def forward(count, core, queries, key_rows, value_rows, grads):
    rows = pltpu.VMEM((CAP, WIN, ATTN), jnp.bfloat16)
    return call(
        forward_kernel,
        (
            pltpu.VMEM((CAP, WIN, H * WIN), jnp.float32),
            pltpu.VMEM((CAP * WIN, ATTN), jnp.bfloat16),
            pltpu.VMEM((CAP * WIN, HALF), jnp.bfloat16),
            pltpu.VMEM((CAP * WIN, D), jnp.bfloat16),
            pltpu.VMEM((1, D), jnp.float32),
            pltpu.VMEM((UNITS, Z, 128), jnp.bfloat16),
        ),
        [smem_spec()] * 2 + [hbm_spec()] * 4,
        (vmem_spec(),) * 6,
        [
            rows, rows, rows, pltpu.SemaphoreType.DMA((4,)),
        ],
        800_000_000,
    )(count, core, *(in_hbm(array) for array in (queries, key_rows, value_rows, grads)))


def own_half(core, attended, grads, bias_row):
    return call(
        own_kernel,
        (
            pltpu.VMEM((UNITS, Z, 128), jnp.bfloat16),
            pltpu.VMEM((CAP * WIN, HALF), jnp.bfloat16),
        ),
        [smem_spec()] + [vmem_spec()] * 3,
        (vmem_spec(),) * 2,
        [],
        300_000_000,
    )(core, *(in_vmem(array) for array in (attended, grads, bias_row)))


def near_half(core, queries, key_rows, value_rows, grads, att_own, near):
    rows = pltpu.VMEM((CAP, WIN, ATTN), jnp.bfloat16)
    return call(
        near_kernel,
        (
            rows, rows, rows, pltpu.VMEM((CAP * WIN, D), jnp.bfloat16),
            pltpu.VMEM((CAP * WIN, HALF), jnp.bfloat16), pltpu.VMEM((CAP * WIN, D), jnp.float32),
            jax.ShapeDtypeStruct((ROWS, D), jnp.float32),
        ),
        [smem_spec()] + [hbm_spec()] * 4 + [vmem_spec()] * 2,
        (vmem_spec(),) * 6 + (hbm_spec(),),
        [
            pltpu.VMEM((HALF, D), jnp.bfloat16), pltpu.VMEM((ROWS, D), jnp.float32),
            pltpu.SemaphoreType.DMA((4,)), pltpu.SemaphoreType.DMA,
        ],
        600_000_000,
    )(
        core, *(in_hbm(array) for array in (queries, key_rows, value_rows, grads)),
        in_vmem(att_own), in_vmem(near),
    )


def backward(count, core, *held):
    rows = jax.ShapeDtypeStruct((CAP, WIN, ATTN), jnp.bfloat16)
    made = pltpu.VMEM((CAP, WIN, ATTN), jnp.bfloat16)
    return call(
        backward_kernel,
        (jax.ShapeDtypeStruct((CAP, WIN, D), jnp.bfloat16), rows, rows, rows),
        [smem_spec()] * 2 + [vmem_spec()] * 9,
        (hbm_spec(),) * 4,
        [
            pltpu.VMEM((CAP, WIN, D), jnp.bfloat16), made, made, made,
            pltpu.VMEM((CAP * WIN, ATTN), jnp.bfloat16), pltpu.VMEM((HALF, D), jnp.bfloat16),
            pltpu.SemaphoreType.DMA((4,)),
        ],
        1_200_000_000,
    )(count, core, *(in_vmem(array) for array in held))


def exchange(blocks, axis):
    return lax.all_to_all(blocks, axis, 0, 0, tiled=True)


def other_core(value):
    return lax.ppermute(value, "c", [(0, 1), (1, 0)])


def added(parts):
    return jnp.sum(parts.astype(jnp.float32), axis=0)


def own_units(proj_weight, proj_bias):
    units = jnp.concatenate(
        [
            proj_weight.reshape(ROWS * BLOCKS, 128),
            jnp.pad(proj_bias, (0, 128 - BIAS))[None],
            jnp.zeros((UNITS - ROWS * BLOCKS - 1, 128), jnp.bfloat16),
        ],
        axis=0,
    )
    mine = lax.axis_index("y") * X + lax.axis_index("x")
    return lax.dynamic_index_in_dim(units.reshape(HELP, PART, 128), mine, 0, keepdims=False)


def on_device(queries, key_rows, value_rows, grad_out, proj_weight, proj_bias, live_count):
    core = lax.axis_index("c").reshape(1)
    grads = grad_out.reshape(CAP * WIN, D)
    share = own_units(proj_weight, proj_bias)
    probs, attended, att_other, held_grads, bias_row, other = forward(
        live_count, core, queries, key_rows, value_rows, grads
    )
    own, att_own = own_half(core, attended, held_grads, bias_row)
    both = added(jnp.stack([own, other_core(other)])).astype(jnp.bfloat16)
    over_help = exchange(both.reshape(HELP, PART, Z, 128), ("y", "x"))
    part = added(over_help).astype(jnp.bfloat16).transpose(1, 0, 2)
    shares = jnp.broadcast_to(share[None], (Z, PART, 128))
    over_z = exchange(jnp.concatenate([part, shares], axis=1), "z")
    whole = added(over_z[:, :PART])
    ends = jnp.pad(whole.astype(jnp.bfloat16), ((0, Z - PART), (0, 0)))[None]
    sent = jnp.concatenate([over_z[:, PART:].transpose(1, 0, 2), ends], axis=0)
    near = exchange(jnp.broadcast_to(sent[None], (HELP, PART + 1, Z, 128)), ("y", "x"))
    *held, first, partial, weight_grad = near_half(
        core, queries, key_rows, value_rows, grads, att_own, near
    )
    encoded, grad_queries, grad_keys, grad_values = backward(
        live_count, core, *held, probs, att_other, first, partial, other_core(near)
    )
    owner, at = divmod(ROWS * BLOCKS, PART)
    bias_grad = near[owner, PART, at, :BIAS].astype(jnp.float32)
    return (encoded, grad_queries, grad_keys, grad_values, weight_grad, bias_grad)


def solution(mesh):
    torus = Mesh(mesh.devices.reshape(Z, CORES, Y, X), ("z", "c", "y", "x"))
    windows = P(("z", "c", "y", "x"), None, None)
    lines, line = P(("z", "c"), None), P(("z", "c"))
    return jax.shard_map(
        on_device,
        mesh=torus,
        in_specs=(windows, windows, windows, windows, lines, line, P(("z", "c", "y", "x"))),
        out_specs=(windows, windows, windows, windows, lines, line),
        check_vma=False,
    )
```

```python
import jax
import jax.numpy as jnp
from jax import lax
from jax.experimental import pallas as pl
from jax.experimental.pallas import tpu as pltpu
from jax.sharding import Mesh
from jax.sharding import PartitionSpec as P

H = 8
HD = 80
WIN = 64
CAP = 5
ATTN = 640
D = 1280
Z, CORES, Y, X = 16, 2, 4, 4
SEQ = Z * CORES
HELP = Y * X
ROWS = ATTN // SEQ
BIAS = D // SEQ
HALF = ATTN // 2
BLOCKS = D // 128
PAIRS = H // 2
SPAN = 256
PART = 13
UNITS = HELP * PART
SCALE = HD**-0.5
VMEM_LIMIT = 24 * 1024 * 1024
NT = (((1,), (1,)), ((), ()))
TN = (((0,), (0,)), ((), ()))
NN = (((1,), (0,)), ((), ()))


def mm(left, right, dims):
    return lax.dot_general(left, right, dims, preferred_element_type=jnp.float32)


def head_masks(pair):
    lane = lax.broadcasted_iota(jnp.int32, (1, SPAN), 1)
    first = 32 * pair
    in_a = (lane >= first) & (lane < first + HD)
    in_b = (lane >= first + HD) & (lane < first + 2 * HD)
    return in_a.astype(jnp.float32), in_b.astype(jnp.float32)


def stacked(rows, mask_a, mask_b):
    return jnp.concatenate(
        [rows * mask_a.astype(jnp.bfloat16), rows * mask_b.astype(jnp.bfloat16)], axis=0
    )


def add_span(tiles, pair, value):
    for part in range(2):
        piece = value[:, 128 * part : 128 * (part + 1)]
        at = pair + part
        tiles[at] = piece if tiles[at] is None else tiles[at] + piece


def bias_pick():
    from_place = lax.broadcasted_iota(jnp.int32, (D, 128), 0)
    to_lane = lax.broadcasted_iota(jnp.int32, (D, 128), 1)
    owner = (from_place * 1639) >> 16
    return jnp.where(from_place - owner * BIAS == to_lane, 1.0, 0.0).astype(jnp.bfloat16)


def bias_owner(core):
    seq = lax.broadcasted_iota(jnp.int32, (Z, D), 0) * CORES + core
    place = lax.broadcasted_iota(jnp.int32, (Z, D), 1)
    return (place >= seq * BIAS) & (place < (seq + 1) * BIAS)


def row_order(core):
    place = lax.broadcasted_iota(jnp.int32, (1, HALF), 1)
    feature = (place & (Z - 1)) * (CORES * ROWS) + core * ROWS + (place >> 4)
    rows = lax.broadcasted_iota(jnp.int32, (ATTN, HALF), 0)
    return jnp.where(rows == feature, 1.0, 0.0).astype(jnp.bfloat16)


def copies(pairs, sems):
    return [
        pltpu.make_async_copy(there, here, sems.at[at]) for at, (there, here) in enumerate(pairs)
    ]


def put_units(wire_ref, made, start):
    for block in range(2):
        for row in range(ROWS):
            wire_ref[row * BLOCKS + start + block] = made[
                Z * row : Z * (row + 1), 128 * block : 128 * (block + 1)
            ].astype(jnp.bfloat16)


def put_bias(wire_ref, bias_row, core):
    owned = jnp.where(bias_owner(core), jnp.broadcast_to(bias_row, (Z, D)), 0.0)
    wire_ref[ROWS * BLOCKS] = mm(owned.astype(jnp.bfloat16), bias_pick(), NN).astype(jnp.bfloat16)
    for unit in range(ROWS * BLOCKS + 1, UNITS):
        wire_ref[unit] = jnp.zeros((Z, 128), jnp.bfloat16)


def take_units(held, weight_ref, core):
    for unit in range(ROWS * BLOCKS):
        owner, at = divmod(unit, PART)
        row, block = divmod(unit, BLOCKS)
        weight_ref[Z * row : Z * (row + 1), 128 * block : 128 * (block + 1)] = held[owner, at]
    owner, at = divmod(ROWS * BLOCKS, PART)
    spread = mm(held[owner, at], bias_pick(), NT)
    return jnp.sum(jnp.where(bias_owner(core), spread, 0.0), axis=0, keepdims=True)


def forward_kernel(
    count_ref, core_ref, q_hbm, k_hbm, v_hbm, g_hbm,
    probs_ref, natural, att_other_ref, g_ref, bias_ref, other_ref,
    q_ref, k_ref, v_ref, in_sems,
):
    count, my_core = count_ref[0], core_ref[0]
    moves = copies(((q_hbm, q_ref), (k_hbm, k_ref), (v_hbm, v_ref), (g_hbm, g_ref)), in_sems)
    for move in moves:
        move.start()
    order_other = row_order(1 - my_core)
    masks = [head_masks(pair) for pair in range(PAIRS)]
    for move in moves[:3]:
        move.wait()
    for w in range(CAP):
        rows = slice(WIN * w, WIN * (w + 1))
        tiles = [None] * (PAIRS + 1)
        for pair in range(PAIRS):
            span = slice(128 * pair, 128 * pair + SPAN)
            mask_a, mask_b = masks[pair]
            q_both = stacked(q_ref[w, :, span], mask_a, mask_b)
            scores = mm(k_ref[w, :, span], q_both, NT) * SCALE
            raised = jnp.exp(scores - jnp.max(scores, axis=0, keepdims=True))
            probs = raised * (1.0 / jnp.sum(raised, axis=0, keepdims=True))
            probs_ref[w, :, 128 * pair : 128 * (pair + 1)] = probs
            both = mm(probs.astype(jnp.bfloat16), v_ref[w, :, span], TN)
            add_span(tiles, pair, both[:WIN] * mask_a + both[WIN:] * mask_b)
        keep = jnp.where(w < count, 1.0, 0.0)
        for at, tile in enumerate(tiles):
            natural[rows, 128 * at : 128 * (at + 1)] = (tile * keep).astype(jnp.bfloat16)
    att_other = mm(natural[...], order_other, NN).astype(jnp.bfloat16)
    att_other_ref[...] = att_other
    row_of = lax.broadcasted_iota(jnp.int32, (16, CAP * WIN), 1)
    live_rows = jnp.where(row_of < count * WIN, 1.0, 0.0).astype(jnp.bfloat16)
    left = jnp.concatenate([att_other.T, live_rows], axis=0)
    moves[3].wait()
    bias_parts = []
    for start in range(0, BLOCKS, 2):
        made = mm(left, g_ref[:, 128 * start : 128 * (start + 2)], NN)
        put_units(other_ref, made, start)
        bias_parts.append(made[HALF : HALF + 1])
    bias_row = jnp.concatenate(bias_parts, axis=1)
    bias_ref[...] = bias_row
    put_bias(other_ref, bias_row, 1 - my_core)


def own_kernel(core_ref, natural, g_ref, bias_ref, own_ref, att_own_ref):
    att_own = mm(natural[...], row_order(core_ref[0]), NN).astype(jnp.bfloat16)
    att_own_ref[...] = att_own
    left = att_own.T
    for start in range(0, BLOCKS, 2):
        put_units(own_ref, mm(left, g_ref[:, 128 * start : 128 * (start + 2)], NN), start)
    put_bias(own_ref, bias_ref[...], core_ref[0])


def near_kernel(
    core_ref, q_hbm, k_hbm, v_hbm, g_hbm, att_own_ref, near_ref,
    q_ref, k_ref, v_ref, g_ref, first_ref, sum_ref, grad_hbm, weight_ref, grad_ref, in_sems,
    out_sem,
):
    moves = copies(((g_hbm, g_ref), (v_hbm, v_ref), (q_hbm, q_ref), (k_hbm, k_ref)), in_sems)
    for move in moves:
        move.start()
    for owner in range(HELP):
        made = near_ref[owner, PART].astype(jnp.float32)
        for at in range(PART):
            row, block = divmod(owner * PART + at, BLOCKS)
            if row < ROWS:
                grad_ref[row : row + 1, 128 * block : 128 * (block + 1)] = made[at : at + 1]
    grad_move = pltpu.make_async_copy(grad_ref, grad_hbm, out_sem)
    grad_move.start()
    bias = take_units(near_ref, weight_ref, core_ref[0])
    for start in range(0, D, SPAN):
        cols = slice(start, start + SPAN)
        sum_ref[:, cols] = mm(att_own_ref[...], weight_ref[:, cols], NN) + bias[:, cols]
    moves[0].wait()
    first_ref[...] = mm(g_ref[...], weight_ref[...], NT).astype(jnp.bfloat16)
    for move in moves[1:]:
        move.wait()
    grad_move.wait()


def backward_kernel(
    count_ref, core_ref, q_ref, k_ref, v_ref, g_ref, probs_ref, att_ref, first_ref, sum_ref,
    far_ref, enc_hbm, dq_hbm, dk_hbm, dv_hbm,
    enc_ref, dq_ref, dk_ref, dv_ref, grad_att, weight_ref, out_sems,
):
    count, my_core = count_ref[0], core_ref[0]
    masks = [head_masks(pair) for pair in range(PAIRS)]
    bias = take_units(far_ref, weight_ref, 1 - my_core)
    second = mm(g_ref[...], weight_ref[...], NT).astype(jnp.bfloat16)
    grad_att[...] = (
        mm(first_ref[...], row_order(my_core), NT) + mm(second, row_order(1 - my_core), NT)
    ).astype(jnp.bfloat16)
    live_rows = lax.broadcasted_iota(jnp.int32, (CAP * WIN, 1), 0) < count * WIN
    for w in range(CAP):
        rows = slice(WIN * w, WIN * (w + 1))
        keep = jnp.where(w < count, 1.0, 0.0)
        dq_tiles, dk_tiles, dv_tiles = ([None] * (PAIRS + 1) for _ in range(3))
        for pair in range(PAIRS):
            span = slice(128 * pair, 128 * pair + SPAN)
            mask_a, mask_b = masks[pair]
            g_both = stacked(grad_att[rows, span], mask_a, mask_b)
            q_both = stacked(q_ref[w, :, span], mask_a, mask_b)
            grad_probs = mm(v_ref[w, :, span], g_both, NT)
            probs = probs_ref[w, :, 128 * pair : 128 * (pair + 1)]
            probs_low = probs.astype(jnp.bfloat16)
            delta = jnp.sum(probs_low.astype(jnp.float32) * grad_probs, axis=0, keepdims=True)
            grad_scores = (probs * (grad_probs - delta)).astype(jnp.bfloat16)
            add_span(dv_tiles, pair, mm(probs_low, g_both, NN))
            add_span(dk_tiles, pair, mm(grad_scores, q_both, NN))
            both = mm(grad_scores, k_ref[w, :, span], TN)
            add_span(dq_tiles, pair, both[:WIN] * mask_a + both[WIN:] * mask_b)
        for at in range(PAIRS + 1):
            cols = slice(128 * at, 128 * (at + 1))
            dq_ref[w, :, cols] = (dq_tiles[at] * (keep * SCALE)).astype(jnp.bfloat16)
            dk_ref[w, :, cols] = (dk_tiles[at] * (keep * SCALE)).astype(jnp.bfloat16)
            dv_ref[w, :, cols] = (dv_tiles[at] * keep).astype(jnp.bfloat16)
        cols = slice(SPAN * w, SPAN * (w + 1))
        encoded = sum_ref[:, cols] + mm(att_ref[...], weight_ref[:, cols], NN) + bias[:, cols]
        encoded = jnp.where(live_rows, encoded, 0.0).astype(jnp.bfloat16)
        for window in range(CAP):
            enc_ref[window, :, cols] = encoded[WIN * window : WIN * (window + 1)]
    back = copies(
        ((enc_ref, enc_hbm), (dq_ref, dq_hbm), (dk_ref, dk_hbm), (dv_ref, dv_hbm)), out_sems
    )
    for move in back:
        move.start()
    for move in back:
        move.wait()


def in_hbm(value):
    return pltpu.with_memory_space_constraint(value, pltpu.HBM)


def in_vmem(value):
    return pltpu.with_memory_space_constraint(value, pltpu.VMEM)


def vmem_spec():
    return pl.BlockSpec(memory_space=pltpu.VMEM)


def hbm_spec():
    return pl.BlockSpec(memory_space=pltpu.HBM)


def smem_spec():
    return pl.BlockSpec(memory_space=pltpu.SMEM)


def call(kernel, out_shape, in_specs, out_specs, scratch_shapes, flops):
    return pl.pallas_call(
        kernel,
        out_shape=out_shape,
        in_specs=in_specs,
        out_specs=out_specs,
        scratch_shapes=scratch_shapes,
        compiler_params=pltpu.CompilerParams(vmem_limit_bytes=VMEM_LIMIT),
        cost_estimate=pl.CostEstimate(flops=flops, bytes_accessed=4_000_000, transcendentals=0),
    )


def forward(count, core, queries, key_rows, value_rows, grads):
    rows = pltpu.VMEM((CAP, WIN, ATTN), jnp.bfloat16)
    return call(
        forward_kernel,
        (
            pltpu.VMEM((CAP, WIN, H * WIN), jnp.float32),
            pltpu.VMEM((CAP * WIN, ATTN), jnp.bfloat16),
            pltpu.VMEM((CAP * WIN, HALF), jnp.bfloat16),
            pltpu.VMEM((CAP * WIN, D), jnp.bfloat16),
            pltpu.VMEM((1, D), jnp.float32),
            pltpu.VMEM((UNITS, Z, 128), jnp.bfloat16),
        ),
        [smem_spec()] * 2 + [hbm_spec()] * 4,
        (vmem_spec(),) * 6,
        [
            rows, rows, rows, pltpu.SemaphoreType.DMA((4,)),
        ],
        800_000_000,
    )(count, core, *(in_hbm(array) for array in (queries, key_rows, value_rows, grads)))


def own_half(core, attended, grads, bias_row):
    return call(
        own_kernel,
        (
            pltpu.VMEM((UNITS, Z, 128), jnp.bfloat16),
            pltpu.VMEM((CAP * WIN, HALF), jnp.bfloat16),
        ),
        [smem_spec()] + [vmem_spec()] * 3,
        (vmem_spec(),) * 2,
        [],
        300_000_000,
    )(core, *(in_vmem(array) for array in (attended, grads, bias_row)))


def near_half(core, queries, key_rows, value_rows, grads, att_own, near):
    rows = pltpu.VMEM((CAP, WIN, ATTN), jnp.bfloat16)
    return call(
        near_kernel,
        (
            rows, rows, rows, pltpu.VMEM((CAP * WIN, D), jnp.bfloat16),
            pltpu.VMEM((CAP * WIN, HALF), jnp.bfloat16), pltpu.VMEM((CAP * WIN, D), jnp.float32),
            jax.ShapeDtypeStruct((ROWS, D), jnp.float32),
        ),
        [smem_spec()] + [hbm_spec()] * 4 + [vmem_spec()] * 2,
        (vmem_spec(),) * 6 + (hbm_spec(),),
        [
            pltpu.VMEM((HALF, D), jnp.bfloat16), pltpu.VMEM((ROWS, D), jnp.float32),
            pltpu.SemaphoreType.DMA((4,)), pltpu.SemaphoreType.DMA,
        ],
        600_000_000,
    )(
        core, *(in_hbm(array) for array in (queries, key_rows, value_rows, grads)),
        in_vmem(att_own), in_vmem(near),
    )


def backward(count, core, *held):
    rows = jax.ShapeDtypeStruct((CAP, WIN, ATTN), jnp.bfloat16)
    made = pltpu.VMEM((CAP, WIN, ATTN), jnp.bfloat16)
    return call(
        backward_kernel,
        (jax.ShapeDtypeStruct((CAP, WIN, D), jnp.bfloat16), rows, rows, rows),
        [smem_spec()] * 2 + [vmem_spec()] * 9,
        (hbm_spec(),) * 4,
        [
            pltpu.VMEM((CAP, WIN, D), jnp.bfloat16), made, made, made,
            pltpu.VMEM((CAP * WIN, ATTN), jnp.bfloat16), pltpu.VMEM((HALF, D), jnp.bfloat16),
            pltpu.SemaphoreType.DMA((4,)),
        ],
        1_200_000_000,
    )(count, core, *(in_vmem(array) for array in held))


def exchange(blocks, axis):
    return lax.all_to_all(blocks, axis, 0, 0, tiled=True)


def other_core(value):
    return lax.ppermute(value, "c", [(0, 1), (1, 0)])


def added(parts):
    return jnp.sum(parts.astype(jnp.float32), axis=0)


def own_units(proj_weight, proj_bias):
    units = jnp.concatenate(
        [
            proj_weight.reshape(ROWS * BLOCKS, 128),
            jnp.pad(proj_bias, (0, 128 - BIAS))[None],
            jnp.zeros((UNITS - ROWS * BLOCKS - 1, 128), jnp.bfloat16),
        ],
        axis=0,
    )
    mine = lax.axis_index("y") * X + lax.axis_index("x")
    return lax.dynamic_index_in_dim(units.reshape(HELP, PART, 128), mine, 0, keepdims=False)


def on_device(queries, key_rows, value_rows, grad_out, proj_weight, proj_bias, live_count):
    core = lax.axis_index("c").reshape(1)
    grads = grad_out.reshape(CAP * WIN, D)
    share = own_units(proj_weight, proj_bias)
    probs, attended, att_other, held_grads, bias_row, other = forward(
        live_count, core, queries, key_rows, value_rows, grads
    )
    own, att_own = own_half(core, attended, held_grads, bias_row)
    both = added(jnp.stack([own, other_core(other)])).astype(jnp.bfloat16)
    both, shares = lax.optimization_barrier((both, jnp.broadcast_to(share[None], (Z, PART, 128))))
    over_help = exchange(both.reshape(HELP, PART, Z, 128), ("y", "x"))
    part = added(over_help).astype(jnp.bfloat16).transpose(1, 0, 2)
    over_z = exchange(jnp.concatenate([part, shares], axis=1), "z")
    whole = added(over_z[:, :PART])
    ends = jnp.pad(whole.astype(jnp.bfloat16), ((0, Z - PART), (0, 0)))[None]
    sent = jnp.concatenate([over_z[:, PART:].transpose(1, 0, 2), ends], axis=0)
    near = exchange(jnp.broadcast_to(sent[None], (HELP, PART + 1, Z, 128)), ("y", "x"))
    *held, first, partial, weight_grad = near_half(
        core, queries, key_rows, value_rows, grads, att_own, near
    )
    encoded, grad_queries, grad_keys, grad_values = backward(
        live_count, core, *held, probs, att_other, first, partial, other_core(near)
    )
    owner, at = divmod(ROWS * BLOCKS, PART)
    bias_grad = near[owner, PART, at, :BIAS].astype(jnp.float32)
    return (encoded, grad_queries, grad_keys, grad_values, weight_grad, bias_grad)


def solution(mesh):
    torus = Mesh(mesh.devices.reshape(Z, CORES, Y, X), ("z", "c", "y", "x"))
    windows = P(("z", "c", "y", "x"), None, None)
    lines, line = P(("z", "c"), None), P(("z", "c"))
    return jax.shard_map(
        on_device,
        mesh=torus,
        in_specs=(windows, windows, windows, windows, lines, line, P(("z", "c", "y", "x"))),
        out_specs=(windows, windows, windows, windows, lines, line),
        check_vma=False,
    )
```
